256 devices in a mesh: corpus: 16 (over z, core), batch: 4 (over x), tensor: 4 (over y).
Axes of the slice: x: 4, y: 4, z: 8, core: 2. Of those that a mesh axis runs over, the one named last changes fastest.
Arguments:
- states: bfloat16 [4, 32, 256, 768], P('batch', 'corpus'), may hold values from -24 to 24
- token_ids: int32 [4, 32, 256], P('batch', 'corpus'), may hold values from 0 to 50264, as said below
- hop_passages: int32 [4, 32], P('batch'), may hold values from 0 to 131071
- path_question: int32 [4, 32], P('batch'), may hold values from 0 to 15, never falling along the last dimension, each value on 1 to 4 neighbouring positions
- question_vecs: bfloat16 [4, 16, 768], P('batch'), may hold values from -2 to 2
- passage_slab: bfloat16 [131072, 768], P(('corpus', 'tensor')), may hold values from -5 to 5
- w_qkv: bfloat16 [768, 3, 768], P(None, None, 'tensor'), may hold values from -0.21875 to 0.21875
- w_out: bfloat16 [768, 768], P('tensor'), may hold values from -0.21875 to 0.21875
- w_up: bfloat16 [768, 3072], P(None, 'tensor'), may hold values from -0.21875 to 0.21875
- w_down: bfloat16 [3072, 768], P('tensor'), may hold values from -0.109375 to 0.109375
- gain_attn: float32 [768], replicated, may hold values from 0.1 to 1.9
- gain_out: float32 [768], replicated, may hold values from 0.1 to 1.9
Outputs:
- log_probs: float32 [4, 16, 131072], P('batch', None, ('corpus', 'tensor'))
The draws below stay inside these ranges and needn't reach their ends.
Inputs may be any that keep to these rules, and one draw needn't show every extreme that they name: `token_ids`: position 0 of every text holds 0; id 1 is padding and fills exactly the positions from a text's length on; lengths run from 64 to 256, and texts 0, 2, 4, ... of each mini-batch have no padding.
All inputs are finite; a program needn't handle non-finite values.
Results may differ from the reference program's by a relative error of at most 0.0012.
Values may be sent and summed in bfloat16 or wider, within the bound.
A program may use at most 64 MiB of HBM per device.

```python
import math
import jax
import jax.numpy as jnp
import numpy as np
from jax import lax

D = 768
HEADS = 12
HEAD_DIM = 64
FF = 3072
VOCAB = 50265
SEQ = 256
HOPS = 4
TXT_DEV = 2
MB = 4
TXT = 32
QB = 16
NPASS = 131072


def first_hop_ids(key):
    return jax.random.randint(jax.random.fold_in(key, 21), (MB, TXT), 0, NPASS, dtype=jnp.int32)


def passage_rows(key, index):
    base_key = jax.random.fold_in(key, 22)

    def one_row(row_index):
        return jnp.clip(jax.random.normal(jax.random.fold_in(base_key, row_index), (D,), jnp.float32), -5.0, 5.0)
    flat_index = index.reshape(-1)
    return jax.vmap(one_row)(flat_index).reshape(index.shape + (D,))


def draw_hop_passages(key, part):
    return first_hop_ids(key)


def draw_passage_slab(key, part):
    return passage_rows(key, jnp.arange(NPASS, dtype=jnp.int32)).astype(jnp.bfloat16)


def draw_question_vecs(key, part):
    key = jax.random.fold_in(key, 31)
    sample = jnp.clip(0.108 * jax.random.normal(key, (MB, QB, D), jnp.float32), -0.6, 0.6)
    return sample.astype(jnp.bfloat16)


def draw_states(key, part):
    key = jax.random.fold_in(key, 1)
    extent = (MB, TXT, SEQ, D)
    sample = jnp.clip(jax.random.normal(key, extent, jnp.float32), -6.0, 6.0)
    return sample.astype(jnp.bfloat16)


def draw_token_ids(key, part):
    key = jax.random.fold_in(key, 2)
    length_key, word_key = jax.random.split(key)
    lengths = jax.random.randint(length_key, (MB, TXT, 1), SEQ // 4, SEQ + 1, dtype=jnp.int32)
    text_index = lax.broadcasted_iota(jnp.int32, (MB, TXT, 1), 1)
    lengths = jnp.where(text_index % TXT_DEV == 0, SEQ, lengths)
    words = jax.random.randint(word_key, (MB, TXT, SEQ), 3, VOCAB, dtype=jnp.int32)
    position = lax.broadcasted_iota(jnp.int32, (MB, TXT, SEQ), 2)
    words = jnp.where(position == 0, 0, words)
    return jnp.where(position >= lengths, 1, words)


def levels(stream_key, dims, pieces, low, high):
    def one(dim, shards_of):
        draws = jax.random.uniform(jax.random.fold_in(jax.random.fold_in(stream_key, 6), dim), (shards_of,), jnp.float32, low / len(pieces), high / len(pieces))
        return jnp.repeat(jnp.exp(draws), dims[dim] // shards_of).reshape((-1,) + (1,) * (len(dims) - dim - 1))

    gain = one(*pieces[0])
    for cut in pieces[1:]:
        gain = gain * one(*cut)
    return gain


def split_up(amount, total, limit, lean):
    weights = [(1 << 20) // math.isqrt(grade ** lean) + 1 for grade in range(2, amount + 1)]
    rest, given = total - limit - (amount - 1), [1] * (amount - 1)
    while rest > 0:
        movable = [i for i in range(amount - 1) if given[i] < limit]
        pool, budget = sum([weights[i] for i in movable]), rest
        for i in movable:
            extra = min(limit - given[i], max(1, budget * weights[i] // pool), rest)
            given[i] = given[i] + extra
            rest = rest - extra
    return np.array([limit] + given)


def ragged_sizes(own_key, number_of, total, reach, slope):
    if number_of == 2:
        one = jax.random.randint(own_key, (), max(1, total - reach), min(reach, total - 1) + 1)
        return jnp.stack([one, total - one])
    sizes = jnp.asarray(split_up(number_of, total, reach, slope), jnp.int32)
    pairs = (number_of - 1) // 2
    donor, taker = sizes[1:1 + 2 * pairs:2], sizes[2:2 + 2 * pairs:2]
    room = jnp.minimum(donor - 1, reach - taker)
    shifted = jax.random.randint(jax.random.fold_in(own_key, 1), (pairs,), 0, 1 << 20) % (room + 1)
    sizes = sizes.at[1:1 + 2 * pairs:2].set(donor - shifted).at[2:2 + 2 * pairs:2].set(taker + shifted)
    return sizes[jax.random.permutation(jax.random.fold_in(own_key, 2), number_of)]


def bell_draw(key, dims, deviation, bound, pieces=(), held_as=jnp.bfloat16):
    array = jax.random.normal(key, dims, jnp.float32) * deviation
    if len(pieces) > 0:
        array = levels(key, dims, pieces, -0.22, 0.18) * array
    return jnp.clip(array, min=-bound, max=bound).astype(held_as)


def setup_inputs(seed: int = 0) -> dict:
    keys = jax.random.split(jax.random.key(seed), 13)
    return {
        "states": draw_states(jax.random.fold_in(keys[12], 71), 0),
        "token_ids": draw_token_ids(jax.random.fold_in(keys[12], 71), 0),
        "hop_passages": draw_hop_passages(jax.random.fold_in(keys[12], 71), 0),
        "path_question": jax.vmap(lambda own: jnp.searchsorted(jnp.cumsum(ragged_sizes(own, QB, TXT, HOPS, 1)), jnp.arange(TXT), side="right"))(jax.random.split(keys[3], MB)).reshape((MB, TXT)).astype(jnp.int32),
        "question_vecs": draw_question_vecs(jax.random.fold_in(keys[12], 71), 0),
        "passage_slab": draw_passage_slab(jax.random.fold_in(keys[12], 71), 0),
        "w_qkv": bell_draw(keys[6], (D, 3, D), D ** -0.5, 0.21875, ((2, 4),)),
        "w_out": bell_draw(keys[7], (D, D), D ** -0.5, 0.21875, ((0, 4),)),
        "w_up": bell_draw(keys[8], (D, FF), D ** -0.5, 0.21875, ((1, 4),)),
        "w_down": bell_draw(keys[9], (FF, D), FF ** -0.5, 0.109375, ((0, 4),)),
        "gain_attn": jnp.clip(1.0 + 0.18 * jax.random.normal(keys[10], (D,), jnp.float32), 0.1, 1.9),
        "gain_out": jnp.clip(1.0 + 0.18 * jax.random.normal(keys[11], (D,), jnp.float32), 0.1, 1.9),
    }


epsilon = 1e-05
score_gain = 3.0

def layer_norm(values, scale_vec):
    centered = values - lax.optimization_barrier(jnp.mean(values, axis=-1, keepdims=True))
    spread = lax.optimization_barrier(jnp.mean(centered * centered, axis=-1, keepdims=True))
    return centered * lax.rsqrt(spread + epsilon) * scale_vec.astype(jnp.float32)

def attend_text(pair_args):
    projected_text, real_text = pair_args
    queries = projected_text[:, 0].astype(jnp.float32)
    key_vecs = projected_text[:, 1].astype(jnp.float32)
    value_vecs = projected_text[:, 2].astype(jnp.float32)
    logits = jnp.einsum('qhd,khd->hqk', queries, key_vecs) * HEAD_DIM ** (-0.5)
    logits = jnp.where(real_text[None, None, :], logits, -jnp.inf)
    largest = lax.optimization_barrier(jnp.max(logits, axis=-1, keepdims=True))
    weights = jnp.exp(logits - largest)
    weights = (weights / lax.optimization_barrier(jnp.sum(weights, axis=-1, keepdims=True))).astype(jnp.bfloat16)
    context = jnp.einsum('hqk,khd->qhd', weights.astype(jnp.float32), value_vecs)
    return context.astype(jnp.bfloat16).reshape(SEQ, HEADS * HEAD_DIM)

def encode_batch(states, token_ids, w_qkv, w_out, w_up, w_down, gain_attn, gain_out):
    text_count = states.shape[0]
    real_token = token_ids != 1
    counts = lax.optimization_barrier(jnp.sum(real_token.astype(jnp.float32), axis=1))
    flat_rows = states.reshape(text_count * SEQ, D)
    projected = jnp.dot(flat_rows, w_qkv.reshape(D, 3 * D), preferred_element_type=jnp.float32).astype(jnp.bfloat16)
    projected = projected.reshape(text_count, SEQ, 3, HEADS, HEAD_DIM)
    context = lax.map(attend_text, (projected, real_token)).reshape(text_count * SEQ, D)
    attended = jnp.dot(context, w_out, preferred_element_type=jnp.float32)
    hidden = layer_norm(flat_rows.astype(jnp.float32) + attended, gain_attn).astype(jnp.bfloat16)
    activated = jax.nn.gelu(jnp.dot(hidden, w_up, preferred_element_type=jnp.float32), approximate=False).astype(jnp.bfloat16)
    fed_forward = jnp.dot(activated, w_down, preferred_element_type=jnp.float32)
    encoded = layer_norm(hidden.astype(jnp.float32) + fed_forward, gain_out).reshape(text_count, SEQ, D)
    pooled = lax.optimization_barrier(jnp.sum(jnp.where(real_token[:, :, None], encoded, 0.0), axis=1)) / counts[:, None]
    return pooled.astype(jnp.bfloat16)

def reference(states, token_ids, hop_passages, path_question, question_vecs, passage_slab, w_qkv, w_out, w_up, w_down, gain_attn, gain_out):
    outputs = []
    for batch_index in range(MB):
        pooled = encode_batch(states[batch_index], token_ids[batch_index], w_qkv, w_out, w_up, w_down, gain_attn, gain_out)
        pooled_wide = pooled.astype(jnp.float32)
        queries = (pooled_wide * lax.rsqrt(lax.optimization_barrier(jnp.sum(pooled_wide * pooled_wide, axis=-1, keepdims=True)) + 1e-06)).astype(jnp.bfloat16)
        hop_rows = jnp.take(passage_slab, hop_passages[batch_index], axis=0).astype(jnp.float32)
        question_rows = jnp.take(question_vecs[batch_index], path_question[batch_index], axis=0).astype(jnp.float32)
        hop_score = lax.optimization_barrier(jnp.sum(hop_rows * question_rows, axis=-1))
        path_scores = hop_score[:, None] + score_gain * jnp.dot(queries, passage_slab.T, preferred_element_type=jnp.float32)
        member = path_question[batch_index][None, :] == jnp.arange(QB, dtype=jnp.int32)[:, None]

        def marginal_of(member_row):
            masked = jnp.where(member_row[:, None], path_scores, -jnp.inf)
            largest = lax.optimization_barrier(jnp.max(masked, axis=0))
            return largest + jnp.log(lax.optimization_barrier(jnp.sum(jnp.exp(masked - largest[None, :]), axis=0)))
        marginal = lax.map(marginal_of, member)
        largest = lax.optimization_barrier(jnp.max(marginal, axis=1, keepdims=True))
        log_norm = largest + jnp.log(lax.optimization_barrier(jnp.sum(jnp.exp(marginal - largest), axis=1, keepdims=True)))
        outputs.append(marginal - log_norm)
    return jnp.stack(outputs)
```

```python
import functools

import jax
import jax.numpy as jnp
from jax import lax
from jax.experimental import pallas as pl
from jax.experimental.pallas import tpu as pltpu
from jax.sharding import PartitionSpec as P

HEAD_DIM = 64
HOPS = 4
MESH = pl.DeviceIdType.MESH
F32 = jnp.float32
BF16 = jnp.bfloat16

epsilon = 1e-05
score_gain = 3.0


def dot(a, b, ca, cb):
    return lax.dot_general(a, b, (((ca,), (cb,)), ((), ())), preferred_element_type=F32)


def layer_norm(values, scale_row):
    centered = values - jnp.mean(values, axis=-1, keepdims=True)
    spread = jnp.mean(centered * centered, axis=-1, keepdims=True)
    return centered * lax.rsqrt(spread + epsilon) * scale_row


def gelu(v):
    return 0.5 * v * (1.0 + lax.erf(v * (0.5 ** 0.5)))


def iota(shape, dim):
    return lax.broadcasted_iota(jnp.int32, shape, dim)


def col_to_row(col, width):
    n = col.shape[0]
    same = iota((n, width), 0) == iota((n, width), 1)
    return jnp.sum(jnp.where(same, col, jnp.zeros_like(col)), axis=0, keepdims=True)


def row_to_col(row, n):
    width = row.shape[1]
    same = iota((n, width), 0) == iota((n, width), 1)
    return jnp.sum(jnp.where(same, row, jnp.zeros_like(row)), axis=1, keepdims=True)


def kernel(
    sizes,
    tok_ref, hop_ref, pq_ref, qv_ref, gain_a_ref, gain_o_ref,
    x_hbm, wqkv_hbm, wout_hbm, wup_hbm, wdown_hbm, slab_hbm,
    out_ref,
    x, wqkv, wout, wup, wdown, slab,
    qkv, ctx, hid, act, ffp, ffr, encs, pool_y, pool_c, hop_y, hop_c, lse_y, lse_c,
    load_sem, w1s, w1r, w2s, w2r, w3s, w3r, cs, cr, fs, fr,
    hys, hyr, hcs, hcr, pys, pyr, pcs, pcr, lys, lyr, lcs, lcr,
):
    n_corpus, n_batch, n_tensor, texts, seq, width = sizes
    c = lax.axis_index("corpus")
    b = lax.axis_index("batch")
    t = lax.axis_index("tensor")
    core = lax.rem(c, 2)
    sibling = c + 1 - 2 * core
    heads_here = wqkv.shape[0] // (3 * HEAD_DIM)
    inner = heads_here * HEAD_DIM
    rows = seq // n_tensor
    ff_here = wup.shape[1]
    passages = slab.shape[0]
    questions = qv_ref.shape[0]
    paths = n_corpus * texts
    own_pass = (c * n_tensor + t) * passages

    def y_peer(d):
        return (c, b, lax.rem(t + d, n_tensor))

    def x_peer(f):
        return (c, lax.rem(b + f, n_batch), t)

    def c_peer(e):
        return (lax.rem(c + e, n_corpus), b, t)

    def remote(src, dst, s, r, dev):
        return pltpu.make_async_remote_copy(
            src_ref=src, dst_ref=dst, send_sem=s, recv_sem=r, device_id=dev, device_id_type=MESH
        )

    loads = []
    for i, (src, dst) in enumerate((
        (x_hbm, x), (wqkv_hbm, wqkv), (wout_hbm, wout.at[0]), (wup_hbm, wup), (wdown_hbm, wdown), (slab_hbm, slab),
    )):
        copy = pltpu.make_async_copy(src, dst, load_sem.at[i])
        copy.start()
        loads.append(copy)
    load_x, load_qkv, load_out, load_up, load_down, load_slab = loads

    barrier = pltpu.get_barrier_semaphore()
    peers = (
        [y_peer(d) for d in range(1, n_tensor)]
        + [x_peer(f) for f in range(1, n_batch)]
        + [c_peer(e) for e in range(1, n_corpus)]
    )
    for dev in peers:
        pl.semaphore_signal(barrier, inc=1, device_id=dev, device_id_type=MESH)
    pl.semaphore_wait(barrier, len(peers))

    piece = inner // n_batch
    half = width // 2
    piece_rows = pl.ds(pl.multiple_of(b * piece, 16), piece)
    half_cols = pl.ds(pl.multiple_of(core * half, 128), half)
    load_out.wait()
    leg1 = [
        remote(
            wout.at[0, piece_rows, half_cols], wout.at[d, piece_rows, half_cols],
            w1s.at[d - 1], w1r.at[d - 1], y_peer(d),
        )
        for d in range(1, n_tensor)
    ]
    for copy in leg1:
        copy.start()

    load_x.wait()
    load_qkv.wait()
    qkv[...] = dot(wqkv[...], x[...], 1, 1).astype(BF16)

    for copy in leg1:
        copy.wait_recv()
    leg2 = [
        remote(
            wout.at[1:n_tensor, piece_rows, half_cols], wout.at[1:n_tensor, piece_rows, half_cols],
            w2s.at[f - 1], w2r.at[f - 1], x_peer(f),
        )
        for f in range(1, n_batch)
    ]
    for copy in leg2:
        copy.start()

    real = tok_ref[...] != 1
    counts = jnp.sum(real.astype(F32), axis=1, keepdims=True)

    ctx_sends = []
    for i in range(texts):
        cols = slice(i * seq, (i + 1) * seq)
        keep = iota((seq, 1), 0).astype(F32) < counts[i:i + 1, :]
        for h in range(heads_here):
            lo = h * HEAD_DIM
            q = qkv[lo:lo + HEAD_DIM, cols] * jnp.asarray(HEAD_DIM ** -0.5, BF16)
            k = qkv[inner + lo:inner + lo + HEAD_DIM, cols]
            v = qkv[2 * inner + lo:2 * inner + lo + HEAD_DIM, cols]
            logits = dot(k, q, 0, 0)
            logits = jnp.where(keep, logits, -jnp.inf)
            weights = jnp.exp(logits - jnp.max(logits, axis=0, keepdims=True))
            weights = (weights * (1.0 / jnp.sum(weights, axis=0, keepdims=True))).astype(BF16)
            ctx[0, i, lo:lo + HEAD_DIM, :] = dot(v, weights, 1, 0).astype(BF16)
        for d in range(1, n_tensor):
            copy = remote(ctx.at[0, i], ctx.at[d, i], cs.at[i, d - 1], cr.at[i, d - 1], y_peer(d))
            copy.start()
            ctx_sends.append(copy)

    for copy in leg2:
        copy.wait_recv()
    leg3 = remote(
        wout.at[1:n_tensor, :, half_cols], wout.at[1:n_tensor, :, half_cols],
        w3s, w3r, (sibling, b, t),
    )
    leg3.start()

    load_slab.wait()
    pq = pq_ref[...]
    member = iota((questions, paths), 0) == pq
    before = jnp.sum((pq < iota((questions, paths), 0)).astype(F32), axis=1, keepdims=True)
    amount = jnp.sum(member.astype(F32), axis=1, keepdims=True)
    hop_col = row_to_col(hop_ref[...].astype(F32), paths)
    here = iota((paths, passages), 1).astype(F32) == hop_col - own_pass.astype(F32)
    picked = dot(here.astype(F32).astype(BF16), slab[...], 1, 0)
    question_rows = dot(member.astype(F32).astype(BF16), qv_ref[...], 0, 0)
    hop_y[0] = col_to_row(jnp.sum(picked * question_rows, axis=1, keepdims=True), 128)
    hop_sends = [
        remote(hop_y.at[0], hop_y.at[d], hys.at[d - 1], hyr.at[d - 1], y_peer(d)) for d in range(1, n_tensor)
    ]
    for copy in hop_sends:
        copy.start()

    leg3.wait_recv()
    load_up.wait()
    load_down.wait()
    ff_sends = []
    for i in range(texts):
        text_rows = slice(i * seq, (i + 1) * seq)
        attended = x[text_rows, :].astype(F32)
        for d in range(n_tensor):
            if d:
                ctx_sends[i * (n_tensor - 1) + d - 1].wait_recv()
            attended = attended + dot(ctx[d, i], wout[d], 0, 0)
        hid[text_rows, :] = layer_norm(attended, gain_a_ref[...]).astype(BF16)
        for n in range(0, ff_here, 256):
            up = dot(hid[text_rows, :], wup[:, n:n + 256], 1, 0)
            act[:, n:n + 256] = gelu(up).astype(BF16)
        ffp[i] = dot(act[...], wdown[...], 1, 0).astype(BF16)
        for d in range(1, n_tensor):
            owner = lax.rem(t + d, n_tensor)
            copy = remote(
                ffp.at[i, pl.ds(pl.multiple_of(owner * rows, 16), rows)], ffr.at[i, d - 1],
                fs.at[i, d - 1], fr.at[i, d - 1], y_peer(d),
            )
            copy.start()
            ff_sends.append(copy)
        if i == 0:
            for copy in hop_sends:
                copy.wait_recv()
            hop_c[0] = jnp.sum(hop_y[...], axis=0)
            hopc_sends = [
                remote(hop_c.at[0], hop_c.at[e], hcs.at[e - 1], hcr, c_peer(e)) for e in range(1, n_corpus)
            ]
            for copy in hopc_sends:
                copy.start()

    for i in range(texts):
        own = pl.ds(pl.multiple_of(t * rows, 16), rows)
        own_hid = pl.ds(pl.multiple_of(i * seq + t * rows, 16), rows)
        total = hid[own_hid, :].astype(F32) + ffp[i, own, :].astype(F32)
        for d in range(1, n_tensor):
            ff_sends[i * (n_tensor - 1) + d - 1].wait_recv()
            total = total + ffr[i, d - 1].astype(F32)
        encoded = layer_norm(total, gain_o_ref[...])
        keep = (t * rows + iota((rows, 1), 0)).astype(F32) < counts[i:i + 1, :]
        pool_y[0, i:i + 1, :] = jnp.sum(jnp.where(keep, encoded, 0.0), axis=0, keepdims=True) / counts[i:i + 1, :]
    pool_sends = [
        remote(pool_y.at[0], pool_y.at[d], pys.at[d - 1], pyr.at[d - 1], y_peer(d)) for d in range(1, n_tensor)
    ]
    for copy in pool_sends:
        copy.start()
    for copy in pool_sends:
        copy.wait_recv()
    pool_c[0] = jnp.sum(pool_y[...], axis=0).astype(BF16).astype(F32)
    poolc_sends = [
        remote(pool_c.at[0], pool_c.at[e], pcs.at[e - 1], pcr, c_peer(e)) for e in range(1, n_corpus)
    ]
    for copy in poolc_sends:
        copy.start()

    rest = n_corpus - 1
    remote(hop_c.at[pl.ds(1, rest)], hop_c.at[pl.ds(1, rest)], hcs.at[0], hcr, c_peer(1)).wait_recv()
    hop_row = jnp.sum(hop_c[...], axis=0)[:, :paths]
    path_at = iota((questions, paths), 1).astype(F32)
    slot = iota((questions, paths), 1)
    slot_path = lax.rem(2 * paths + texts * c - slot + 2 * lax.rem(slot, texts), paths).astype(F32)
    hops, valid, picks = [], [], []
    for k in range(HOPS):
        ok = amount > k
        hops.append(jnp.sum(jnp.where(path_at == before + k, hop_row, 0.0), axis=1, keepdims=True))
        valid.append(ok)
        picks.append(jnp.where((slot_path == before + k) & ok, 1.0, 0.0))
    pick = jnp.concatenate(picks, axis=0).astype(BF16)

    remote(pool_c.at[pl.ds(1, rest)], pool_c.at[pl.ds(1, rest)], pcs.at[0], pcr, c_peer(1)).wait_recv()
    pooled = pool_c[...].reshape(paths, width)
    queries = (pooled * lax.rsqrt(jnp.sum(pooled * pooled, axis=-1, keepdims=True) + 1e-06)).astype(BF16)
    chosen = dot(pick, queries, 1, 0).astype(BF16)
    direct = dot(chosen, slab[...], 1, 1)
    scores = [
        jnp.where(valid[k], hops[k] + score_gain * direct[k * questions:(k + 1) * questions], -jnp.inf)
        for k in range(HOPS)
    ]
    top = functools.reduce(jnp.maximum, scores)
    marginal = top + jnp.log(sum(jnp.exp(s - top) for s in scores))
    local_top = jnp.max(marginal, axis=1, keepdims=True)
    local_lse = local_top + jnp.log(jnp.sum(jnp.exp(marginal - local_top), axis=1, keepdims=True))

    lse_y[0] = col_to_row(local_lse, 128)
    lse_sends = [
        remote(lse_y.at[0], lse_y.at[d], lys.at[d - 1], lyr.at[d - 1], y_peer(d)) for d in range(1, n_tensor)
    ]
    for copy in lse_sends:
        copy.start()
    for copy in lse_sends:
        copy.wait_recv()
    parts = lse_y[...]
    most = jnp.max(parts, axis=0)
    lse_c[0] = most + jnp.log(jnp.sum(jnp.exp(parts - most[None]), axis=0))
    lsec_sends = [
        remote(lse_c.at[0], lse_c.at[e], lcs.at[e - 1], lcr, c_peer(e)) for e in range(1, n_corpus)
    ]
    for copy in lsec_sends:
        copy.start()
    remote(lse_c.at[pl.ds(1, rest)], lse_c.at[pl.ds(1, rest)], lcs.at[0], lcr, c_peer(1)).wait_recv()
    parts = lse_c[...]
    most = jnp.max(parts, axis=0)
    norm = most + jnp.log(jnp.sum(jnp.exp(parts - most[None]), axis=0))
    out_ref[...] = marginal - row_to_col(norm, questions)

    leg3.wait_send()
    for group in (leg1, leg2, ctx_sends, hop_sends, hopc_sends, ff_sends, pool_sends, poolc_sends, lse_sends, lsec_sends):
        for copy in group:
            copy.wait_send()


def shards(mesh_sizes, states, token_ids, hop_passages, path_question, question_vecs, passage_slab,
           w_qkv, w_out, w_up, w_down, gain_attn, gain_out):
    n_corpus, n_batch, n_tensor = mesh_sizes
    texts, seq, width = states.shape[1:]
    total = texts * seq
    passages = passage_slab.shape[0]
    questions = question_vecs.shape[1]
    inner = w_qkv.shape[2]
    ff_here = w_up.shape[1]
    sizes = (n_corpus, n_batch, n_tensor, texts, seq, width)
    ny, nx, nc = n_tensor - 1, n_batch - 1, n_corpus - 1
    dma = pltpu.SemaphoreType.DMA
    vmem = pl.BlockSpec(memory_space=pltpu.VMEM)
    hbm = pl.BlockSpec(memory_space=pl.ANY)
    result = pl.pallas_call(
        functools.partial(kernel, sizes),
        out_shape=jax.ShapeDtypeStruct((questions, passages), F32),
        in_specs=[vmem] * 6 + [hbm] * 6,
        out_specs=vmem,
        scratch_shapes=[
            pltpu.VMEM((total, width), BF16),
            pltpu.VMEM((3 * inner, width), BF16),
            pltpu.VMEM((n_tensor, inner, width), BF16),
            pltpu.VMEM((width, ff_here), BF16),
            pltpu.VMEM((ff_here, width), BF16),
            pltpu.VMEM((passages, width), BF16),
            pltpu.VMEM((3 * inner, total), BF16),
            pltpu.VMEM((n_tensor, texts, inner, seq), BF16),
            pltpu.VMEM((total, width), BF16),
            pltpu.VMEM((seq, ff_here), BF16),
            pltpu.VMEM((texts, seq, width), BF16),
            pltpu.VMEM((texts, ny, seq // n_tensor, width), BF16),
            pltpu.VMEM((8, 128), F32),
            pltpu.VMEM((n_tensor, texts, width), F32),
            pltpu.VMEM((n_corpus, texts, width), F32),
            pltpu.VMEM((n_tensor, 1, 128), F32),
            pltpu.VMEM((n_corpus, 1, 128), F32),
            pltpu.VMEM((n_tensor, 1, 128), F32),
            pltpu.VMEM((n_corpus, 1, 128), F32),
            dma((6,)),
            dma((ny,)), dma((ny,)), dma((nx,)), dma((nx,)), dma, dma,
            dma((texts, ny)), dma((texts, ny)), dma((texts, ny)), dma((texts, ny)),
            dma((ny,)), dma((ny,)), dma((nc,)), dma,
            dma((ny,)), dma((ny,)), dma((nc,)), dma,
            dma((ny,)), dma((ny,)), dma((nc,)), dma,
        ],
        compiler_params=pltpu.CompilerParams(
            collective_id=0, has_side_effects=True, vmem_limit_bytes=48 * 1024 * 1024
        ),
        name="hop_two",
    )(
        token_ids[0], hop_passages, path_question, question_vecs[0],
        gain_attn[None], gain_out[None],
        states.reshape(total, width), jnp.transpose(w_qkv, (1, 2, 0)).reshape(3 * inner, width),
        w_out, w_up, w_down, passage_slab,
    )
    return result[None]


def solution(mesh):
    mesh_sizes = (mesh.shape["corpus"], mesh.shape["batch"], mesh.shape["tensor"])
    return jax.shard_map(
        functools.partial(shards, mesh_sizes),
        mesh=mesh,
        in_specs=(
            P("batch", "corpus", None, None),
            P("batch", "corpus", None),
            P("batch", None),
            P("batch", None),
            P("batch", None, None),
            P(("corpus", "tensor"), None),
            P(None, None, "tensor"),
            P("tensor", None),
            P(None, "tensor"),
            P("tensor", None),
            P(),
            P(),
        ),
        out_specs=P("batch", None, ("corpus", "tensor")),
        check_vma=False,
    )
```

```python
import functools

import jax
import jax.numpy as jnp
from jax import lax
from jax.experimental import pallas as pl
from jax.experimental.pallas import tpu as pltpu
from jax.sharding import PartitionSpec as P

HEAD_DIM = 64
HOPS = 4
PIECE = 128
MESH = pl.DeviceIdType.MESH
F32 = jnp.float32
BF16 = jnp.bfloat16

epsilon = 1e-05
score_gain = 3.0


def dot(a, b, ca, cb):
    return lax.dot_general(a, b, (((ca,), (cb,)), ((), ())), preferred_element_type=F32)


def layer_norm(values, scale_row):
    centered = values - jnp.mean(values, axis=-1, keepdims=True)
    spread = jnp.mean(centered * centered, axis=-1, keepdims=True)
    return centered * lax.rsqrt(spread + epsilon) * scale_row


def gelu(v):
    return 0.5 * v * (1.0 + lax.erf(v * (0.5 ** 0.5)))


def iota(shape, dim):
    return lax.broadcasted_iota(jnp.int32, shape, dim)


def col_to_row(col, width):
    n = col.shape[0]
    same = iota((n, width), 0) == iota((n, width), 1)
    return jnp.sum(jnp.where(same, col, jnp.zeros_like(col)), axis=0, keepdims=True)


def row_to_col(row, n):
    width = row.shape[1]
    same = iota((n, width), 0) == iota((n, width), 1)
    return jnp.sum(jnp.where(same, row, jnp.zeros_like(row)), axis=1, keepdims=True)


def kernel(
    sizes,
    tok_hbm, hop_hbm, pq_hbm, qv_hbm, gain_a_hbm, gain_o_hbm,
    x_hbm, wqkv_hbm, wout_hbm, wup_hbm, wdown_hbm, slab_hbm,
    out_ref,
    tok_ref, hop_ref, pq_ref, qv_ref, gain_a_ref, gain_o_ref,
    x, wqkv, wout, wup, wdown, slab,
    qkv, ctx, hid, act, ffp, ffr, pool_y, pool_c, hop_y, hop_c, lse,
    load_sem, w1s, w1r, w2s, w2r, cs, cr, fs, fr,
    hys, hyr, hcs, hcr, pys, pyr, pcs, pcr, ls, lr, known,
):
    n_corpus, n_batch, n_tensor, texts, seq, width = sizes
    c = lax.axis_index("corpus")
    b = lax.axis_index("batch")
    t = lax.axis_index("tensor")
    core = lax.rem(c, 2)
    sibling = c + 1 - 2 * core
    heads_here = wqkv.shape[0] // (3 * HEAD_DIM)
    inner = heads_here * HEAD_DIM
    ff_here = wup.shape[1]
    passages = slab.shape[0]
    questions = qv_ref.shape[0]
    paths = n_corpus * texts
    piece = ctx.shape[-1]
    own_pass = (c * n_tensor + t) * passages

    def y_peer(d):
        return (c, b, lax.rem(t + d, n_tensor))

    def c_peer(e, d=0):
        return (lax.rem(c + e, n_corpus), b, lax.rem(t + d, n_tensor))

    def chips_away(e):
        return min(e // 2, (n_corpus - e) // 2)

    def remote(src, dst, s, r, dev):
        return pltpu.make_async_remote_copy(
            src_ref=src, dst_ref=dst, send_sem=s, recv_sem=r, device_id=dev, device_id_type=MESH
        )

    def wait_all(buf, sem):
        there = buf.at[pl.ds(1, buf.shape[0] - 1)]
        remote(there, there, sem, sem, y_peer(1)).wait_recv()

    far_first = sorted(range(1, n_corpus), key=lambda e: -chips_away(e))
    far_first_all = sorted(
        [(e, d) for e in range(n_corpus) for d in range(n_tensor) if e or d],
        key=lambda p: -chips_away(p[0]) - min(p[1], n_tensor - p[1]),
    )

    barrier = pltpu.get_barrier_semaphore()
    peers = [y_peer(d) for d in range(1, n_tensor)] + [(sibling, b, lax.rem(t + d, n_tensor)) for d in range(n_tensor)]
    peers += [c_peer(2), c_peer(n_corpus - 2)]
    for dev in peers:
        pl.semaphore_signal(barrier, inc=1, device_id=dev, device_id_type=MESH)

    def tell(stage, chips):
        for e in (2 * chips, n_corpus - 2 * chips):
            pl.semaphore_signal(known.at[stage], inc=1, device_id=c_peer(e), device_id_type=MESH)

    loads = []
    for i, (src, dst) in enumerate((
        (x_hbm, x), (wqkv_hbm, wqkv), (wout_hbm, wout.at[0]), (tok_hbm, tok_ref), (gain_a_hbm, gain_a_ref),
        (gain_o_hbm, gain_o_ref), (hop_hbm, hop_ref), (pq_hbm, pq_ref), (qv_hbm, qv_ref),
        (slab_hbm, slab), (wup_hbm, wup), (wdown_hbm, wdown),
    )):
        loads.append(pltpu.make_async_copy(src, dst, load_sem.at[i]))
    load_x, load_qkv = loads[:2]
    load_small = loads[2:9]
    load_slab, load_up, load_down = loads[9:]
    for copy in loads[:9]:
        copy.start()
    pl.semaphore_wait(barrier, len(peers))

    half = width // 2
    half_cols = pl.ds(pl.multiple_of(core * half, 128), half)
    leg1 = [
        remote(wout_hbm.at[:, half_cols], wout.at[d, :, half_cols], w1s.at[d - 1], w1r.at[d - 1], y_peer(d))
        for d in range(1, n_tensor)
    ]
    for copy in leg1:
        copy.start()
    tell(0, 1)

    load_x.wait()
    load_qkv.wait()
    for copy in (load_slab, load_up, load_down):
        copy.start()
    qkv[...] = dot(wqkv[...], x[...], 1, 1).astype(BF16)
    for copy in load_small:
        copy.wait()
    gain_a = jnp.concatenate([gain_a_ref[r:r + 1, :] for r in range(width // 128)], axis=1)
    gain_o = jnp.concatenate([gain_o_ref[r:r + 1, :] for r in range(width // 128)], axis=1)
    real = tok_ref[...] != 1
    counts = jnp.sum(real.astype(F32), axis=1, keepdims=True)

    split = seq // piece
    ctx_sends = []
    for i in range(texts):
        cols = slice(i * seq, (i + 1) * seq)
        keep = iota((seq, 1), 0).astype(F32) < counts[i:i + 1, :]
        for h in range(heads_here):
            lo = h * HEAD_DIM
            q = qkv[lo:lo + HEAD_DIM, cols] * jnp.asarray(HEAD_DIM ** -0.5, BF16)
            k = qkv[inner + lo:inner + lo + HEAD_DIM, cols]
            v = qkv[2 * inner + lo:2 * inner + lo + HEAD_DIM, cols]
            logits = dot(k, q, 0, 0)
            logits = jnp.where(keep, logits, -jnp.inf)
            weights = jnp.exp(logits - jnp.max(logits, axis=0, keepdims=True))
            weights = (weights * (1.0 / jnp.sum(weights, axis=0, keepdims=True))).astype(BF16)
            context = dot(v, weights, 1, 0).astype(BF16)
            for j in range(split):
                ctx[0, i * split + j, lo:lo + HEAD_DIM, :] = context[:, j * piece:(j + 1) * piece]
        for p in range(i * split, (i + 1) * split):
            group = [
                remote(ctx.at[0, p], ctx.at[d, p], cs.at[p, d - 1], cr.at[p, d - 1], y_peer(d))
                for d in range(1, n_tensor)
            ]
            for copy in group:
                copy.start()
            ctx_sends.append(group)

    pl.semaphore_wait(known.at[0], 2)
    tell(1, 2)

    load_slab.wait()
    pq = pq_ref[...]
    member = iota((questions, paths), 0) == pq
    before = jnp.sum((pq < iota((questions, paths), 0)).astype(F32), axis=1, keepdims=True)
    amount = jnp.sum(member.astype(F32), axis=1, keepdims=True)
    hop_col = row_to_col(hop_ref[...].astype(F32), paths)
    here = iota((paths, passages), 1).astype(F32) == hop_col - own_pass.astype(F32)
    picked = dot(here.astype(F32).astype(BF16), slab[...], 1, 0)
    question_rows = dot(member.astype(F32).astype(BF16), qv_ref[...], 0, 0)
    hop_y[0] = col_to_row(jnp.sum(picked * question_rows, axis=1, keepdims=True), 128)
    hop_sends = [
        remote(hop_y.at[0], hop_y.at[d], hys.at[d - 1], hyr, y_peer(d)) for d in range(1, n_tensor)
    ]
    for copy in hop_sends:
        copy.start()

    leg2 = []
    for d in (1, n_tensor - 1, 2):
        if d == 2:
            pl.semaphore_wait(known.at[1], 2)
            tell(2, 1)
        leg1[d - 1].wait_recv()
        copy = remote(wout.at[d, :, half_cols], wout.at[d, :, half_cols], w2s.at[d - 1], w2r.at[d - 1], (sibling, b, t))
        copy.start()
        leg2.append(copy)
    load_up.wait()
    load_down.wait()
    for copy in leg2:
        copy.wait_recv()

    rows = piece // n_tensor
    ff_sends = []
    for p in range(texts * split):
        piece_rows = slice(p * piece, (p + 1) * piece)
        attended = x[piece_rows, :].astype(F32)
        for d in range(n_tensor):
            if d:
                ctx_sends[p][d - 1].wait_recv()
            attended = attended + dot(ctx[d, p], wout[d], 0, 0)
        hid[piece_rows, :] = layer_norm(attended, gain_a).astype(BF16)
        for n in range(0, ff_here, 256):
            up = dot(hid[piece_rows, :], wup[:, n:n + 256], 1, 0)
            act[:, n:n + 256] = gelu(up).astype(BF16)
        ffp[p] = dot(act[...], wdown[...], 1, 0).astype(BF16)
        group = []
        for d in range(1, n_tensor):
            owner = lax.rem(t + d, n_tensor)
            copy = remote(
                ffp.at[p, pl.ds(pl.multiple_of(owner * rows, 16), rows)], ffr.at[p, d - 1],
                fs.at[p, d - 1], fr.at[p], y_peer(d),
            )
            copy.start()
            group.append(copy)
        ff_sends.append(group)
        if p == 0:
            pl.semaphore_wait(known.at[2], 2)
            wait_all(hop_y, hyr)
            hop_c[0] = jnp.sum(hop_y[...], axis=0)
            hopc_sends = [
                remote(hop_c.at[0], hop_c.at[e], hcs.at[e - 1], hcr, c_peer(e)) for e in far_first
            ]
            for copy in hopc_sends:
                copy.start()

    sums = [None] * texts
    for p in range(texts * split):
        i, j = p // split, p % split
        own = pl.ds(pl.multiple_of(t * rows, 16), rows)
        own_hid = pl.ds(pl.multiple_of(p * piece + t * rows, 16), rows)
        remote(ffr.at[p], ffr.at[p], fs.at[p, 0], fr.at[p], y_peer(1)).wait_recv()
        total = hid[own_hid, :].astype(F32) + ffp[p, own, :].astype(F32)
        for d in range(1, n_tensor):
            total = total + ffr[p, d - 1].astype(F32)
        encoded = layer_norm(total, gain_o)
        keep = (j * piece + t * rows + iota((rows, 1), 0)).astype(F32) < counts[i:i + 1, :]
        part = jnp.sum(jnp.where(keep, encoded, 0.0), axis=0, keepdims=True)
        sums[i] = part if sums[i] is None else sums[i] + part
    pool_y[0] = jnp.concatenate(sums, axis=0) / counts
    pool_sends = [
        remote(pool_y.at[0], pool_y.at[d], pys.at[d - 1], pyr, y_peer(d)) for d in range(1, n_tensor)
    ]
    for copy in pool_sends:
        copy.start()
    wait_all(pool_y, pyr)
    pool_c[0] = jnp.sum(pool_y[...], axis=0).astype(BF16).astype(F32)
    poolc_sends = [
        remote(pool_c.at[0], pool_c.at[e], pcs.at[e - 1], pcr, c_peer(e)) for e in far_first
    ]
    for copy in poolc_sends:
        copy.start()

    wait_all(hop_c, hcr)
    hop_row = jnp.sum(hop_c[...], axis=0)[:, :paths]
    path_at = iota((questions, paths), 1).astype(F32)
    slot = iota((questions, paths), 1)
    slot_path = lax.rem(2 * paths + texts * c - slot + 2 * lax.rem(slot, texts), paths).astype(F32)
    hops, valid, picks = [], [], []
    for k in range(HOPS):
        ok = amount > k
        hops.append(jnp.sum(jnp.where(path_at == before + k, hop_row, 0.0), axis=1, keepdims=True))
        valid.append(ok)
        picks.append(jnp.where((slot_path == before + k) & ok, 1.0, 0.0))
    pick = jnp.concatenate(picks, axis=0).astype(BF16)

    wait_all(pool_c, pcr)
    pooled = pool_c[...].reshape(paths, width)
    queries = (pooled * lax.rsqrt(jnp.sum(pooled * pooled, axis=-1, keepdims=True) + 1e-06)).astype(BF16)
    chosen = dot(pick, queries, 1, 0).astype(BF16)
    direct = dot(chosen, slab[...], 1, 1)
    scores = [
        jnp.where(valid[k], hops[k] + score_gain * direct[k * questions:(k + 1) * questions], -jnp.inf)
        for k in range(HOPS)
    ]
    top = functools.reduce(jnp.maximum, scores)
    marginal = top + jnp.log(sum(jnp.exp(s - top) for s in scores))
    local_top = jnp.max(marginal, axis=1, keepdims=True)
    local_lse = local_top + jnp.log(jnp.sum(jnp.exp(marginal - local_top), axis=1, keepdims=True))

    lse[0] = col_to_row(local_lse, 128)
    lse_sends = [
        remote(lse.at[0], lse.at[k + 1], ls.at[k], lr, c_peer(e, d)) for k, (e, d) in enumerate(far_first_all)
    ]
    for copy in lse_sends:
        copy.start()
    wait_all(lse, lr)
    parts = lse[...]
    most = jnp.max(parts, axis=0)
    norm = most + jnp.log(jnp.sum(jnp.exp(parts - most[None]), axis=0))
    out_ref[...] = marginal - row_to_col(norm, questions)

    for group in [leg1, leg2, hop_sends, hopc_sends, pool_sends, poolc_sends, lse_sends] + ctx_sends + ff_sends:
        for copy in group:
            copy.wait_send()


def shards(mesh_sizes, states, token_ids, hop_passages, path_question, question_vecs, passage_slab,
           w_qkv, w_out, w_up, w_down, gain_attn, gain_out):
    n_corpus, n_batch, n_tensor = mesh_sizes
    texts, seq, width = states.shape[1:]
    total = texts * seq
    passages = passage_slab.shape[0]
    questions = question_vecs.shape[1]
    inner = w_qkv.shape[2]
    ff_here = w_up.shape[1]
    sizes = (n_corpus, n_batch, n_tensor, texts, seq, width)
    ny, nc = n_tensor - 1, n_corpus - 1
    pieces = total // PIECE
    dma = pltpu.SemaphoreType.DMA
    vmem = pl.BlockSpec(memory_space=pltpu.VMEM)
    hbm = pl.BlockSpec(memory_space=pl.ANY)
    result = pl.pallas_call(
        functools.partial(kernel, sizes),
        out_shape=jax.ShapeDtypeStruct((questions, passages), F32),
        in_specs=[hbm] * 12,
        out_specs=vmem,
        scratch_shapes=[
            pltpu.VMEM((texts, seq), jnp.int32),
            pltpu.VMEM((1, n_corpus * texts), jnp.int32),
            pltpu.VMEM((1, n_corpus * texts), jnp.int32),
            pltpu.VMEM((questions, width), BF16),
            pltpu.VMEM((width // 128, 128), F32),
            pltpu.VMEM((width // 128, 128), F32),
            pltpu.VMEM((total, width), BF16),
            pltpu.VMEM((3 * inner, width), BF16),
            pltpu.VMEM((n_tensor, inner, width), BF16),
            pltpu.VMEM((width, ff_here), BF16),
            pltpu.VMEM((ff_here, width), BF16),
            pltpu.VMEM((passages, width), BF16),
            pltpu.VMEM((3 * inner, total), BF16),
            pltpu.VMEM((n_tensor, pieces, inner, PIECE), BF16),
            pltpu.VMEM((total, width), BF16),
            pltpu.VMEM((PIECE, ff_here), BF16),
            pltpu.VMEM((pieces, PIECE, width), BF16),
            pltpu.VMEM((pieces, ny, PIECE // n_tensor, width), BF16),
            pltpu.VMEM((n_tensor, texts, width), F32),
            pltpu.VMEM((n_corpus, texts, width), F32),
            pltpu.VMEM((n_tensor, 1, 128), F32),
            pltpu.VMEM((n_corpus, 1, 128), F32),
            pltpu.VMEM((n_tensor * n_corpus, 1, 128), F32),
            dma((12,)),
            dma((ny,)), dma((ny,)), dma((ny,)), dma((ny,)),
            dma((pieces, ny)), dma((pieces, ny)), dma((pieces, ny)), dma((pieces,)),
            dma((ny,)), dma, dma((nc,)), dma,
            dma((ny,)), dma, dma((nc,)), dma,
            dma((n_tensor * n_corpus - 1,)), dma,
            pltpu.SemaphoreType.REGULAR((3,)),
        ],
        compiler_params=pltpu.CompilerParams(
            collective_id=0, has_side_effects=True, vmem_limit_bytes=60 * 1024 * 1024
        ),
        name="hop_two",
    )(
        token_ids[0], hop_passages, path_question, question_vecs[0],
        gain_attn.reshape(-1, 128), gain_out.reshape(-1, 128),
        states.reshape(total, width), jnp.transpose(w_qkv, (1, 2, 0)).reshape(3 * inner, width),
        w_out, w_up, w_down, passage_slab,
    )
    return result[None]


def solution(mesh):
    mesh_sizes = (mesh.shape["corpus"], mesh.shape["batch"], mesh.shape["tensor"])
    return jax.shard_map(
        functools.partial(shards, mesh_sizes),
        mesh=mesh,
        in_specs=(
            P("batch", "corpus", None, None),
            P("batch", "corpus", None),
            P("batch", None),
            P("batch", None),
            P("batch", None, None),
            P(("corpus", "tensor"), None),
            P(None, None, "tensor"),
            P("tensor", None),
            P(None, "tensor"),
            P("tensor", None),
            P(),
            P(),
        ),
        out_specs=P("batch", None, ("corpus", "tensor")),
        check_vma=False,
    )
```

```python
import functools

import jax
import jax.numpy as jnp
from jax import lax
from jax.experimental import pallas as pl
from jax.experimental.pallas import tpu as pltpu
from jax.sharding import PartitionSpec as P

HEAD_DIM = 64
HOPS = 4
PIECE = 128
MESH = pl.DeviceIdType.MESH
F32 = jnp.float32
BF16 = jnp.bfloat16

epsilon = 1e-05
score_gain = 3.0


def dot(a, b, ca, cb):
    return lax.dot_general(a, b, (((ca,), (cb,)), ((), ())), preferred_element_type=F32)


def layer_norm(values, scale_row):
    centered = values - jnp.mean(values, axis=-1, keepdims=True)
    spread = jnp.mean(centered * centered, axis=-1, keepdims=True)
    return centered * lax.rsqrt(spread + epsilon) * scale_row


def gelu(v):
    return 0.5 * v * (1.0 + lax.erf(v * (0.5 ** 0.5)))


def iota(shape, dim):
    return lax.broadcasted_iota(jnp.int32, shape, dim)


def col_to_row(col, width):
    n = col.shape[0]
    same = iota((n, width), 0) == iota((n, width), 1)
    return jnp.sum(jnp.where(same, col, jnp.zeros_like(col)), axis=0, keepdims=True)


def row_to_col(row, n):
    width = row.shape[1]
    same = iota((n, width), 0) == iota((n, width), 1)
    return jnp.sum(jnp.where(same, row, jnp.zeros_like(row)), axis=1, keepdims=True)


def kernel(
    sizes,
    tok_hbm, hop_hbm, pq_hbm, qv_hbm, gain_a_hbm, gain_o_hbm,
    x_hbm, wqkv_hbm, wout_hbm, wup_hbm, wdown_hbm, slab_hbm,
    out_ref,
    tok_ref, hop_ref, pq_ref, qv_ref, gain_a_ref, gain_o_ref,
    x, wqkv, wout, wup, wdown, slab,
    qkv, ctx, hid, act, ffp, ffr, pool_y, pool_c, hop_y, hop_c, lse,
    load_sem, w1s, w1r, w2s, w2r, w3s, w3r, cs, cr, fs, fr,
    hys, hyr, hcs, hcr, pys, pyr, pcs, pcr, ls, lr, known,
):
    n_corpus, n_batch, n_tensor, texts, seq, width = sizes
    c = lax.axis_index("corpus")
    b = lax.axis_index("batch")
    t = lax.axis_index("tensor")
    core = lax.rem(c, 2)
    sibling = c + 1 - 2 * core
    heads_here = wqkv.shape[0] // (3 * HEAD_DIM)
    inner = heads_here * HEAD_DIM
    ff_here = wup.shape[1]
    passages = slab.shape[0]
    questions = qv_ref.shape[0]
    paths = n_corpus * texts
    piece = ctx.shape[-1]
    own_pass = (c * n_tensor + t) * passages

    def y_peer(d):
        return (c, b, lax.rem(t + d, n_tensor))

    def c_peer(e, d=0):
        return (lax.rem(c + e, n_corpus), b, lax.rem(t + d, n_tensor))

    def x_peer(f):
        return (c, lax.rem(b + f, n_batch), t)

    def chips_away(e):
        return min(e // 2, (n_corpus - e) // 2)

    def remote(src, dst, s, r, dev):
        return pltpu.make_async_remote_copy(
            src_ref=src, dst_ref=dst, send_sem=s, recv_sem=r, device_id=dev, device_id_type=MESH
        )

    def wait_all(buf, sem):
        there = buf.at[pl.ds(1, buf.shape[0] - 1)]
        remote(there, there, sem, sem, y_peer(1)).wait_recv()

    far_first = sorted(range(1, n_corpus), key=lambda e: -chips_away(e))
    far_first_all = sorted(
        [(e, d) for e in range(n_corpus) for d in range(n_tensor) if e or d],
        key=lambda p: -chips_away(p[0]) - min(p[1], n_tensor - p[1]),
    )

    barrier = pltpu.get_barrier_semaphore()
    peers = [y_peer(d) for d in range(1, n_tensor)] + [(sibling, b, lax.rem(t + d, n_tensor)) for d in range(n_tensor)]
    peers += [c_peer(2), c_peer(n_corpus - 2), x_peer(1), x_peer(n_batch - 1)]
    for dev in peers:
        pl.semaphore_signal(barrier, inc=1, device_id=dev, device_id_type=MESH)

    def tell(stage, chips):
        for e in (2 * chips, n_corpus - 2 * chips):
            pl.semaphore_signal(known.at[stage], inc=1, device_id=c_peer(e), device_id_type=MESH)

    loads = []
    for i, (src, dst) in enumerate((
        (x_hbm, x), (wqkv_hbm, wqkv), (wout_hbm, wout.at[0]), (tok_hbm, tok_ref), (gain_a_hbm, gain_a_ref),
        (gain_o_hbm, gain_o_ref), (hop_hbm, hop_ref), (pq_hbm, pq_ref), (qv_hbm, qv_ref),
        (slab_hbm, slab), (wup_hbm, wup), (wdown_hbm, wdown),
    )):
        loads.append(pltpu.make_async_copy(src, dst, load_sem.at[i]))
    load_x, load_qkv = loads[:2]
    load_small = loads[2:9]
    load_slab, load_up, load_down = loads[9:]
    for copy in loads[:9]:
        copy.start()
    pl.semaphore_wait(barrier, len(peers))

    half = width // 2
    half_cols = pl.ds(pl.multiple_of(core * half, 128), half)
    other_cols = pl.ds(pl.multiple_of((1 - core) * half, 128), half)
    odd = lax.rem(b, 2)
    quarter = inner // 4
    own_rows = pl.ds(pl.multiple_of(odd * 2 * quarter, 16), 2 * quarter)
    own_part = [pl.ds(pl.multiple_of(odd * 2 * quarter + k * quarter, 16), quarter) for k in range(2)]
    next_part = [pl.ds(pl.multiple_of((1 - odd) * 2 * quarter + k * quarter, 16), quarter) for k in range(2)]
    leg1 = [
        remote(wout_hbm.at[own_rows, half_cols], wout.at[d, own_rows, half_cols], w1s.at[d - 1], w1r.at[d - 1], y_peer(d))
        for d in range(1, n_tensor)
    ]
    for copy in leg1:
        copy.start()
    tell(0, 1)

    load_x.wait()
    load_qkv.wait()
    for copy in (load_slab, load_up, load_down):
        copy.start()
    qkv[...] = dot(wqkv[...], x[...], 1, 1).astype(BF16)
    for copy in load_small:
        copy.wait()
    gain_a = jnp.concatenate([gain_a_ref[r:r + 1, :] for r in range(width // 128)], axis=1)
    gain_o = jnp.concatenate([gain_o_ref[r:r + 1, :] for r in range(width // 128)], axis=1)
    real = tok_ref[...] != 1
    counts = jnp.sum(real.astype(F32), axis=1, keepdims=True)

    split = seq // piece
    ctx_sends = []
    for i in range(texts):
        cols = slice(i * seq, (i + 1) * seq)
        keep = iota((seq, 1), 0).astype(F32) < counts[i:i + 1, :]
        for h in range(heads_here):
            lo = h * HEAD_DIM
            q = qkv[lo:lo + HEAD_DIM, cols] * jnp.asarray(HEAD_DIM ** -0.5, BF16)
            k = qkv[inner + lo:inner + lo + HEAD_DIM, cols]
            v = qkv[2 * inner + lo:2 * inner + lo + HEAD_DIM, cols]
            logits = dot(k, q, 0, 0)
            logits = jnp.where(keep, logits, -jnp.inf)
            weights = jnp.exp(logits - jnp.max(logits, axis=0, keepdims=True))
            weights = (weights * (1.0 / jnp.sum(weights, axis=0, keepdims=True))).astype(BF16)
            context = dot(v, weights, 1, 0).astype(BF16)
            for j in range(split):
                ctx[0, i * split + j, lo:lo + HEAD_DIM, :] = context[:, j * piece:(j + 1) * piece]
        for p in range(i * split, (i + 1) * split):
            group = [
                remote(ctx.at[0, p], ctx.at[d, p], cs.at[p, d - 1], cr.at[p, d - 1], y_peer(d))
                for d in range(1, n_tensor)
            ]
            ctx_sends.append(group)

    def issue(p):
        for copy in ctx_sends[p]:
            copy.start()

    pl.semaphore_wait(known.at[0], 2)
    tell(1, 2)

    issue(0)
    issue(1)
    load_slab.wait()
    pq = pq_ref[...]
    member = iota((questions, paths), 0) == pq
    before = jnp.sum((pq < iota((questions, paths), 0)).astype(F32), axis=1, keepdims=True)
    amount = jnp.sum(member.astype(F32), axis=1, keepdims=True)
    hop_col = row_to_col(hop_ref[...].astype(F32), paths)
    here = iota((paths, passages), 1).astype(F32) == hop_col - own_pass.astype(F32)
    picked = dot(here.astype(F32).astype(BF16), slab[...], 1, 0)
    question_rows = dot(member.astype(F32).astype(BF16), qv_ref[...], 0, 0)
    hop_y[0] = col_to_row(jnp.sum(picked * question_rows, axis=1, keepdims=True), 128)
    hop_sends = [
        remote(hop_y.at[0], hop_y.at[d], hys.at[d - 1], hyr, y_peer(d)) for d in range(1, n_tensor)
    ]
    for copy in hop_sends:
        copy.start()

    leg2 = []
    for d in (1, n_tensor - 1, 2):
        if d == 2:
            pl.semaphore_wait(known.at[1], 2)
            tell(2, 1)
        leg1[d - 1].wait_recv()
        group = [
            remote(wout.at[d, own_part[k], half_cols], wout.at[d, own_part[k], half_cols], w2s.at[d - 1, k], w2r.at[k], x_peer(f))
            for k, f in ((0, 1), (1, n_batch - 1))
        ]
        group.append(remote(wout.at[d, own_rows, half_cols], wout.at[d, own_rows, half_cols], w2s.at[d - 1, 2], w3r, (sibling, b, t)))
        for copy in group:
            copy.start()
        leg2 += group
    issue(2)
    issue(3)
    load_up.wait()
    load_down.wait()

    for k, f in ((0, 1), (1, n_batch - 1)):
        there = wout.at[1:n_tensor, next_part[k], half_cols]
        remote(there, there, w2s.at[0, k], w2r.at[k], x_peer(f)).wait_recv()
        copy = remote(there, there, w3s.at[k], w3r, (sibling, b, t))
        copy.start()
        leg2.append(copy)
    there = wout.at[1:n_tensor, :, other_cols]
    remote(there, there, w3s.at[0], w3r, (sibling, b, t)).wait_recv()


    rows = piece // n_tensor
    ff_sends = []
    for p in range(texts * split):
        piece_rows = slice(p * piece, (p + 1) * piece)
        attended = x[piece_rows, :].astype(F32)
        for d in range(n_tensor):
            if d:
                ctx_sends[p][d - 1].wait_recv()
            attended = attended + dot(ctx[d, p], wout[d], 0, 0)
        hid[piece_rows, :] = layer_norm(attended, gain_a).astype(BF16)
        for n in range(0, ff_here, 256):
            up = dot(hid[piece_rows, :], wup[:, n:n + 256], 1, 0)
            act[:, n:n + 256] = gelu(up).astype(BF16)
        ffp[p] = dot(act[...], wdown[...], 1, 0).astype(BF16)
        group = []
        for d in range(1, n_tensor):
            owner = lax.rem(t + d, n_tensor)
            copy = remote(
                ffp.at[p, pl.ds(pl.multiple_of(owner * rows, 16), rows)], ffr.at[p, d - 1],
                fs.at[p, d - 1], fr.at[p], y_peer(d),
            )
            copy.start()
            group.append(copy)
        ff_sends.append(group)
        if p == 0:
            pl.semaphore_wait(known.at[2], 2)
            wait_all(hop_y, hyr)
            hop_c[0] = jnp.sum(hop_y[...], axis=0)
            hopc_sends = [
                remote(hop_c.at[0], hop_c.at[e], hcs.at[e - 1], hcr, c_peer(e)) for e in far_first
            ]
            for copy in hopc_sends:
                copy.start()

    sums = [None] * texts
    for p in range(texts * split):
        i, j = p // split, p % split
        own = pl.ds(pl.multiple_of(t * rows, 16), rows)
        own_hid = pl.ds(pl.multiple_of(p * piece + t * rows, 16), rows)
        remote(ffr.at[p], ffr.at[p], fs.at[p, 0], fr.at[p], y_peer(1)).wait_recv()
        total = hid[own_hid, :].astype(F32) + ffp[p, own, :].astype(F32)
        for d in range(1, n_tensor):
            total = total + ffr[p, d - 1].astype(F32)
        encoded = layer_norm(total, gain_o)
        keep = (j * piece + t * rows + iota((rows, 1), 0)).astype(F32) < counts[i:i + 1, :]
        part = jnp.sum(jnp.where(keep, encoded, 0.0), axis=0, keepdims=True)
        sums[i] = part if sums[i] is None else sums[i] + part
    pool_y[0] = jnp.concatenate(sums, axis=0) / counts
    pool_sends = [
        remote(pool_y.at[0], pool_y.at[d], pys.at[d - 1], pyr, y_peer(d)) for d in range(1, n_tensor)
    ]
    for copy in pool_sends:
        copy.start()
    wait_all(pool_y, pyr)
    pool_c[0] = jnp.sum(pool_y[...], axis=0).astype(BF16).astype(F32)
    poolc_sends = [
        remote(pool_c.at[0], pool_c.at[e], pcs.at[e - 1], pcr, c_peer(e)) for e in far_first
    ]
    for copy in poolc_sends:
        copy.start()

    wait_all(hop_c, hcr)
    hop_row = jnp.sum(hop_c[...], axis=0)[:, :paths]
    path_at = iota((questions, paths), 1).astype(F32)
    slot = iota((questions, paths), 1)
    slot_path = lax.rem(2 * paths + texts * c - slot + 2 * lax.rem(slot, texts), paths).astype(F32)
    hops, valid, picks = [], [], []
    for k in range(HOPS):
        ok = amount > k
        hops.append(jnp.sum(jnp.where(path_at == before + k, hop_row, 0.0), axis=1, keepdims=True))
        valid.append(ok)
        picks.append(jnp.where((slot_path == before + k) & ok, 1.0, 0.0))
    pick = jnp.concatenate(picks, axis=0).astype(BF16)

    wait_all(pool_c, pcr)
    pooled = pool_c[...].reshape(paths, width)
    queries = (pooled * lax.rsqrt(jnp.sum(pooled * pooled, axis=-1, keepdims=True) + 1e-06)).astype(BF16)
    chosen = dot(pick, queries, 1, 0).astype(BF16)
    direct = dot(chosen, slab[...], 1, 1)
    scores = [
        jnp.where(valid[k], hops[k] + score_gain * direct[k * questions:(k + 1) * questions], -jnp.inf)
        for k in range(HOPS)
    ]
    top = functools.reduce(jnp.maximum, scores)
    marginal = top + jnp.log(sum(jnp.exp(s - top) for s in scores))
    local_top = jnp.max(marginal, axis=1, keepdims=True)
    local_lse = local_top + jnp.log(jnp.sum(jnp.exp(marginal - local_top), axis=1, keepdims=True))

    lse[0] = col_to_row(local_lse, 128)
    lse_sends = [
        remote(lse.at[0], lse.at[k + 1], ls.at[k], lr, c_peer(e, d)) for k, (e, d) in enumerate(far_first_all)
    ]
    for copy in lse_sends:
        copy.start()
    wait_all(lse, lr)
    parts = lse[...]
    most = jnp.max(parts, axis=0)
    norm = most + jnp.log(jnp.sum(jnp.exp(parts - most[None]), axis=0))
    out_ref[...] = marginal - row_to_col(norm, questions)

    for group in [leg1, leg2, hop_sends, hopc_sends, pool_sends, poolc_sends, lse_sends] + ctx_sends[0:] + ff_sends:
        for copy in group:
            copy.wait_send()


def shards(mesh_sizes, states, token_ids, hop_passages, path_question, question_vecs, passage_slab,
           w_qkv, w_out, w_up, w_down, gain_attn, gain_out):
    n_corpus, n_batch, n_tensor = mesh_sizes
    texts, seq, width = states.shape[1:]
    total = texts * seq
    passages = passage_slab.shape[0]
    questions = question_vecs.shape[1]
    inner = w_qkv.shape[2]
    ff_here = w_up.shape[1]
    sizes = (n_corpus, n_batch, n_tensor, texts, seq, width)
    ny, nc = n_tensor - 1, n_corpus - 1
    pieces = total // PIECE
    dma = pltpu.SemaphoreType.DMA
    vmem = pl.BlockSpec(memory_space=pltpu.VMEM)
    hbm = pl.BlockSpec(memory_space=pl.ANY)
    result = pl.pallas_call(
        functools.partial(kernel, sizes),
        out_shape=jax.ShapeDtypeStruct((questions, passages), F32),
        in_specs=[hbm] * 12,
        out_specs=vmem,
        scratch_shapes=[
            pltpu.VMEM((texts, seq), jnp.int32),
            pltpu.VMEM((1, n_corpus * texts), jnp.int32),
            pltpu.VMEM((1, n_corpus * texts), jnp.int32),
            pltpu.VMEM((questions, width), BF16),
            pltpu.VMEM((width // 128, 128), F32),
            pltpu.VMEM((width // 128, 128), F32),
            pltpu.VMEM((total, width), BF16),
            pltpu.VMEM((3 * inner, width), BF16),
            pltpu.VMEM((n_tensor, inner, width), BF16),
            pltpu.VMEM((width, ff_here), BF16),
            pltpu.VMEM((ff_here, width), BF16),
            pltpu.VMEM((passages, width), BF16),
            pltpu.VMEM((3 * inner, total), BF16),
            pltpu.VMEM((n_tensor, pieces, inner, PIECE), BF16),
            pltpu.VMEM((total, width), BF16),
            pltpu.VMEM((PIECE, ff_here), BF16),
            pltpu.VMEM((pieces, PIECE, width), BF16),
            pltpu.VMEM((pieces, ny, PIECE // n_tensor, width), BF16),
            pltpu.VMEM((n_tensor, texts, width), F32),
            pltpu.VMEM((n_corpus, texts, width), F32),
            pltpu.VMEM((n_tensor, 1, 128), F32),
            pltpu.VMEM((n_corpus, 1, 128), F32),
            pltpu.VMEM((n_tensor * n_corpus, 1, 128), F32),
            dma((12,)),
            dma((ny,)), dma((ny,)), dma((ny, 3)), dma((2,)), dma((2,)), dma,
            dma((pieces, ny)), dma((pieces, ny)), dma((pieces, ny)), dma((pieces,)),
            dma((ny,)), dma, dma((nc,)), dma,
            dma((ny,)), dma, dma((nc,)), dma,
            dma((n_tensor * n_corpus - 1,)), dma,
            pltpu.SemaphoreType.REGULAR((3,)),
        ],
        compiler_params=pltpu.CompilerParams(
            collective_id=0, has_side_effects=True, vmem_limit_bytes=60 * 1024 * 1024
        ),
        name="hop_two",
    )(
        token_ids[0], hop_passages, path_question, question_vecs[0],
        gain_attn.reshape(-1, 128), gain_out.reshape(-1, 128),
        states.reshape(total, width), jnp.transpose(w_qkv, (1, 2, 0)).reshape(3 * inner, width),
        w_out, w_up, w_down, passage_slab,
    )
    return result[None]


def solution(mesh):
    mesh_sizes = (mesh.shape["corpus"], mesh.shape["batch"], mesh.shape["tensor"])
    return jax.shard_map(
        functools.partial(shards, mesh_sizes),
        mesh=mesh,
        in_specs=(
            P("batch", "corpus", None, None),
            P("batch", "corpus", None),
            P("batch", None),
            P("batch", None),
            P("batch", None, None),
            P(("corpus", "tensor"), None),
            P(None, None, "tensor"),
            P("tensor", None),
            P(None, "tensor"),
            P("tensor", None),
            P(),
            P(),
        ),
        out_specs=P("batch", None, ("corpus", "tensor")),
        check_vma=False,
    )
```

```python
import functools

import jax
import jax.numpy as jnp
from jax import lax
from jax.experimental import pallas as pl
from jax.experimental.pallas import tpu as pltpu
from jax.sharding import PartitionSpec as P

HEAD_DIM = 64
HOPS = 4
PIECE = 128
MESH = pl.DeviceIdType.MESH
F32 = jnp.float32
BF16 = jnp.bfloat16

epsilon = 1e-05
score_gain = 3.0


def dot(a, b, ca, cb):
    return lax.dot_general(a, b, (((ca,), (cb,)), ((), ())), preferred_element_type=F32)


def layer_norm(values, scale_row):
    centered = values - jnp.mean(values, axis=-1, keepdims=True)
    spread = jnp.mean(centered * centered, axis=-1, keepdims=True)
    return centered * lax.rsqrt(spread + epsilon) * scale_row


def gelu(v):
    return 0.5 * v * (1.0 + lax.erf(v * (0.5 ** 0.5)))


def iota(shape, dim):
    return lax.broadcasted_iota(jnp.int32, shape, dim)


def col_to_row(col, width):
    n = col.shape[0]
    same = iota((n, width), 0) == iota((n, width), 1)
    return jnp.sum(jnp.where(same, col, jnp.zeros_like(col)), axis=0, keepdims=True)


def row_to_col(row, n):
    width = row.shape[1]
    same = iota((n, width), 0) == iota((n, width), 1)
    return jnp.sum(jnp.where(same, row, jnp.zeros_like(row)), axis=1, keepdims=True)


def kernel(
    sizes,
    tok_hbm, hop_hbm, pq_hbm, qv_hbm, gain_a_hbm, gain_o_hbm,
    x_hbm, wqkv_hbm, wout_hbm, wup_hbm, wdown_hbm, slab_hbm,
    out_ref,
    tok_ref, hop_ref, pq_ref, qv_ref, gain_a_ref, gain_o_ref,
    x, wqkv, wout, wup, wdown, slab, slab_t,
    qkv, ctx, hid, act, ffp, ffr, opp, partial, pool, hop_y, hop_c, lse,
    load_sem, w1s, w1r, w2s, w2r, w3s, w3r, cs, cr, fs, fr, oppr,
    hys, hyr, hcs, hcr, ps, pr, ls, lr, known,
):
    n_corpus, n_batch, n_tensor, texts, seq, width = sizes
    c = lax.axis_index("corpus")
    b = lax.axis_index("batch")
    t = lax.axis_index("tensor")
    core = lax.rem(c, 2)
    sibling = c + 1 - 2 * core
    heads_here = wqkv.shape[0] // (3 * HEAD_DIM)
    inner = heads_here * HEAD_DIM
    ff_here = wup.shape[1]
    passages = slab.shape[0]
    questions = qv_ref.shape[0]
    paths = n_corpus * texts
    piece = ctx.shape[-1]
    own_pass = (c * n_tensor + t) * passages

    def y_peer(d):
        return (c, b, lax.rem(t + d, n_tensor))

    def c_peer(e, d=0):
        return (lax.rem(c + e, n_corpus), b, lax.rem(t + d, n_tensor))

    def x_peer(f):
        return (c, lax.rem(b + f, n_batch), t)

    def chips_away(e):
        return min(e // 2, (n_corpus - e) // 2)

    def remote(src, dst, s, r, dev):
        return pltpu.make_async_remote_copy(
            src_ref=src, dst_ref=dst, send_sem=s, recv_sem=r, device_id=dev, device_id_type=MESH
        )

    def wait_all(buf, sem):
        there = buf.at[pl.ds(1, buf.shape[0] - 1)]
        remote(there, there, sem, sem, y_peer(1)).wait_recv()

    far_first = sorted(range(1, n_corpus), key=lambda e: -chips_away(e))
    far_first_all = sorted(
        [(e, d) for e in range(n_corpus) for d in range(n_tensor) if e or d],
        key=lambda p: -chips_away(p[0]) - min(p[1], n_tensor - p[1]),
    )

    barrier = pltpu.get_barrier_semaphore()
    peers = [y_peer(d) for d in range(1, n_tensor)] + [(sibling, b, lax.rem(t + d, n_tensor)) for d in range(n_tensor)]
    peers += [c_peer(2), c_peer(n_corpus - 2), x_peer(1), x_peer(n_batch - 1)]
    for dev in peers:
        pl.semaphore_signal(barrier, inc=1, device_id=dev, device_id_type=MESH)

    def tell(stage, chips):
        for e in (2 * chips, n_corpus - 2 * chips):
            pl.semaphore_signal(known.at[stage], inc=1, device_id=c_peer(e), device_id_type=MESH)

    loads = []
    for i, (src, dst) in enumerate((
        (x_hbm, x), (wqkv_hbm, wqkv), (wout_hbm, wout.at[0]), (tok_hbm, tok_ref), (gain_a_hbm, gain_a_ref),
        (gain_o_hbm, gain_o_ref), (hop_hbm, hop_ref), (pq_hbm, pq_ref), (qv_hbm, qv_ref),
        (slab_hbm, slab), (wup_hbm, wup), (wdown_hbm, wdown),
    )):
        loads.append(pltpu.make_async_copy(src, dst, load_sem.at[i]))
    load_x, load_qkv = loads[:2]
    load_small = loads[2:9]
    load_slab, load_up, load_down = loads[9:]
    for copy in loads[:9]:
        copy.start()
    pl.semaphore_wait(barrier, len(peers))

    half = width // 2
    half_cols = pl.ds(pl.multiple_of(core * half, 128), half)
    other_cols = pl.ds(pl.multiple_of((1 - core) * half, 128), half)
    odd = lax.rem(b, 2)
    quarter = inner // 4
    own_rows = pl.ds(pl.multiple_of(odd * 2 * quarter, 16), 2 * quarter)
    own_part = [pl.ds(pl.multiple_of(odd * 2 * quarter + k * quarter, 16), quarter) for k in range(2)]
    next_part = [pl.ds(pl.multiple_of((1 - odd) * 2 * quarter + k * quarter, 16), quarter) for k in range(2)]
    leg1 = [
        remote(wout_hbm.at[own_rows, half_cols], wout.at[d, own_rows, half_cols], w1s.at[d - 1], w1r.at[d - 1], y_peer(d))
        for d in range(1, n_tensor)
    ]
    for copy in leg1:
        copy.start()
    tell(0, 1)

    load_x.wait()
    load_qkv.wait()
    for copy in (load_slab, load_up, load_down):
        copy.start()
    qkv[...] = dot(wqkv[...], x[...], 1, 1).astype(BF16)
    for copy in load_small:
        copy.wait()
    gain_a = jnp.concatenate([gain_a_ref[r:r + 1, :] for r in range(width // 128)], axis=1)
    gain_o = jnp.concatenate([gain_o_ref[r:r + 1, :] for r in range(width // 128)], axis=1)
    real = tok_ref[...] != 1
    counts = jnp.sum(real.astype(F32), axis=1, keepdims=True)

    split = seq // piece
    for i in range(texts):
        cols = slice(i * seq, (i + 1) * seq)
        keep = iota((seq, 1), 0).astype(F32) < counts[i:i + 1, :]
        for h in range(heads_here):
            lo = h * HEAD_DIM
            q = qkv[lo:lo + HEAD_DIM, cols] * jnp.asarray(HEAD_DIM ** -0.5, BF16)
            k = qkv[inner + lo:inner + lo + HEAD_DIM, cols]
            v = qkv[2 * inner + lo:2 * inner + lo + HEAD_DIM, cols]
            logits = dot(k, q, 0, 0)
            logits = jnp.where(keep, logits, -jnp.inf)
            weights = jnp.exp(logits - jnp.max(logits, axis=0, keepdims=True))
            weights = (weights * (1.0 / jnp.sum(weights, axis=0, keepdims=True))).astype(BF16)
            context = dot(v, weights, 1, 0).astype(BF16)
            for j in range(split):
                ctx[0, i * split + j, lo:lo + HEAD_DIM, :] = context[:, j * piece:(j + 1) * piece]
    steps = (2, 1, 3, 0)
    ctx_sends = {}
    for k in steps:
        ctx_sends[k] = []
        for d in range(1, n_tensor):
            q = lax.rem(t + d + k, n_tensor)
            ctx_sends[k].append(remote(ctx.at[0, q], ctx.at[d, k], cs.at[k, d - 1], cr.at[k, d - 1], y_peer(d)))

    def issue(p):
        for copy in ctx_sends[p]:
            copy.start()

    pl.semaphore_wait(known.at[0], 2)
    tell(1, 2)

    for k in steps:
        issue(k)
    load_slab.wait()
    pq = pq_ref[...]
    member = iota((questions, paths), 0) == pq
    before = jnp.sum((pq < iota((questions, paths), 0)).astype(F32), axis=1, keepdims=True)
    amount = jnp.sum(member.astype(F32), axis=1, keepdims=True)
    hop_col = row_to_col(hop_ref[...].astype(F32), paths)
    here = iota((paths, passages), 1).astype(F32) == hop_col - own_pass.astype(F32)
    picked = dot(here.astype(F32).astype(BF16), slab[...], 1, 0)
    question_rows = dot(member.astype(F32).astype(BF16), qv_ref[...], 0, 0)
    hop_y[0] = col_to_row(jnp.sum(picked * question_rows, axis=1, keepdims=True), 128)
    hop_sends = [
        remote(hop_y.at[0], hop_y.at[d], hys.at[d - 1], hyr, y_peer(d)) for d in range(1, n_tensor)
    ]
    for copy in hop_sends:
        copy.start()

    leg2 = []
    for d in (1, n_tensor - 1, 2):
        if d == 2:
            pl.semaphore_wait(known.at[1], 2)
            tell(2, 1)
        leg1[d - 1].wait_recv()
        group = [
            remote(wout.at[d, own_part[k], half_cols], wout.at[d, own_part[k], half_cols], w2s.at[d - 1, k], w2r.at[k], x_peer(f))
            for k, f in ((0, 1), (1, n_batch - 1))
        ]
        group.append(remote(wout.at[d, own_rows, half_cols], wout.at[d, own_rows, half_cols], w2s.at[d - 1, 2], w3r, (sibling, b, t)))
        for copy in group:
            copy.start()
        leg2 += group
    for n in range(0, passages, 256):
        slab_t[:, n:n + 256] = slab[n:n + 256, :].T
    load_up.wait()
    load_down.wait()

    for k, f in ((0, 1), (1, n_batch - 1)):
        there = wout.at[1:n_tensor, next_part[k], half_cols]
        remote(there, there, w2s.at[0, k], w2r.at[k], x_peer(f)).wait_recv()
        copy = remote(there, there, w3s.at[k], w3r, (sibling, b, t))
        copy.start()
        leg2.append(copy)
    there = wout.at[1:n_tensor, :, other_cols]
    remote(there, there, w3s.at[0], w3r, (sibling, b, t)).wait_recv()


    ff_sends = []
    halves = (slice(0, piece // 2), slice(piece // 2, piece))
    for k in steps:
        q = lax.rem(t + k, n_tensor)
        attended = x[pl.ds(pl.multiple_of(q * piece, 16), piece), :].astype(F32)
        attended = attended + dot(ctx[0, q], wout[0], 0, 0)
        for d in range(1, n_tensor):
            ctx_sends[k][d - 1].wait_recv()
            attended = attended + dot(ctx[d, k], wout[d], 0, 0)
        hidden = layer_norm(attended, gain_a).astype(BF16)
        hid[...] = hidden
        for n in range(0, ff_here, 256):
            up = dot(hid[...], wup[:, n:n + 256], 1, 0)
            act[:, n:n + 256] = gelu(up).astype(BF16)
        down = dot(act[...], wdown[...], 1, 0)
        if k == 2:
            ffp[1] = down.astype(BF16)
            for r, f in ((0, 1), (1, n_tensor - 1)):
                ff_sends.append(remote(ffp.at[1, halves[r]], opp.at[r], fs.at[1, r], oppr.at[r], y_peer(f)))
                ff_sends[-1].start()
        elif k:
            late = 0 if k == 1 else 1
            ffp[k - 1, halves[1 - late], :] = down[halves[1 - late], :].astype(BF16)
            partial[late] = down[halves[late], :]
            part = halves[1 - late]
            ff_sends.append(remote(ffp.at[k - 1, part], ffr.at[k - 1, part], fs.at[k - 1, 1 - late], fr.at[k - 1], y_peer(k)))
            ff_sends[-1].start()
        if k == steps[0]:
            pl.semaphore_wait(known.at[2], 2)
            wait_all(hop_y, hyr)
            hop_c[0] = jnp.sum(hop_y[...], axis=0)
            hopc_sends = [
                remote(hop_c.at[0], hop_c.at[e], hcs.at[e - 1], hcr, c_peer(e)) for e in far_first
            ]
            for copy in hopc_sends:
                copy.start()

    for late, k in ((0, 1), (1, n_tensor - 1)):
        part = halves[late]
        ff_sends[late].wait_recv()
        ffp[k - 1, part, :] = (partial[late] + opp[late].astype(F32)).astype(BF16)
        ff_sends.append(remote(ffp.at[k - 1, part], ffr.at[k - 1, part], fs.at[k - 1, late], fr.at[k - 1], y_peer(k)))
        ff_sends[-1].start()
    total = hid[...].astype(F32) + down
    for k in (1, n_tensor - 1):
        remote(ffr.at[k - 1], ffr.at[k - 1], fs.at[k - 1, 0], fr.at[k - 1], y_peer(k)).wait_recv()
        total = total + ffr[k - 1].astype(F32)
    encoded = layer_norm(total, gain_o)
    own_count = sum(jnp.where(t // split == i, counts[i:i + 1, :], 0.0) for i in range(texts))
    keep = (lax.rem(t, split) * piece + iota((piece, 1), 0)).astype(F32) < own_count
    me = c * n_tensor + t
    pool[pl.ds(me, 1)] = (jnp.sum(jnp.where(keep, encoded, 0.0), axis=0, keepdims=True) / own_count)[None]
    pool_sends = [
        remote(pool.at[me], pool.at[me], ps.at[k], pr, c_peer(e, d)) for k, (e, d) in enumerate(far_first_all)
    ]
    for copy in pool_sends:
        copy.start()

    wait_all(hop_c, hcr)
    hop_row = jnp.sum(hop_c[...], axis=0)[:, :paths]
    path_at = iota((questions, paths), 1).astype(F32)
    hops, picks = [], []
    for k in range(HOPS):
        ok = amount > k
        hop = jnp.sum(jnp.where(path_at == before + k, hop_row, 0.0), axis=1, keepdims=True)
        hops.append(jnp.where(ok, hop, -jnp.inf))
        picks.append(jnp.where((path_at == before + k) & ok, 1.0, 0.0))
    pick = jnp.concatenate(picks, axis=0).astype(BF16)

    others = pool.at[pl.ds(0, n_corpus * n_tensor - 1)]
    remote(others, others, ps.at[0], pr, y_peer(1)).wait_recv()
    pooled = jnp.sum(pool[...].reshape(paths, split, 1, width), axis=1).reshape(paths, width)
    pooled = pooled.astype(BF16).astype(F32)
    queries = (pooled * lax.rsqrt(jnp.sum(pooled * pooled, axis=-1, keepdims=True) + 1e-06)).astype(BF16)
    chosen = dot(pick, queries, 1, 0).astype(BF16)
    direct = dot(chosen, slab_t[...], 1, 0)
    scores = [hops[k] + score_gain * direct[k * questions:(k + 1) * questions] for k in range(HOPS)]
    top = functools.reduce(jnp.maximum, scores)
    inner_sum = sum(jnp.exp(s - top) for s in scores)
    local_top = jnp.max(top, axis=1, keepdims=True)
    local_sum = jnp.sum(inner_sum * jnp.exp(top - local_top), axis=1, keepdims=True)
    local_lse = local_top + jnp.log(local_sum)

    lse[0] = col_to_row(local_lse, 128)
    lse_sends = [
        remote(lse.at[0], lse.at[k + 1], ls.at[k], lr, c_peer(e, d)) for k, (e, d) in enumerate(far_first_all)
    ]
    for copy in lse_sends:
        copy.start()
    marginal = top + jnp.log(inner_sum)
    wait_all(lse, lr)
    parts = lse[...]
    most = jnp.max(parts, axis=0)
    norm = most + jnp.log(jnp.sum(jnp.exp(parts - most[None]), axis=0))
    out_ref[...] = marginal - row_to_col(norm, questions)

    for group in [leg1, leg2, hop_sends, hopc_sends, pool_sends, lse_sends, ff_sends] + list(ctx_sends.values()):
        for copy in group:
            copy.wait_send()


def shards(mesh_sizes, states, token_ids, hop_passages, path_question, question_vecs, passage_slab,
           w_qkv, w_out, w_up, w_down, gain_attn, gain_out):
    n_corpus, n_batch, n_tensor = mesh_sizes
    texts, seq, width = states.shape[1:]
    total = texts * seq
    passages = passage_slab.shape[0]
    questions = question_vecs.shape[1]
    inner = w_qkv.shape[2]
    ff_here = w_up.shape[1]
    sizes = (n_corpus, n_batch, n_tensor, texts, seq, width)
    ny, nc = n_tensor - 1, n_corpus - 1
    pieces = total // PIECE
    dma = pltpu.SemaphoreType.DMA
    vmem = pl.BlockSpec(memory_space=pltpu.VMEM)
    hbm = pl.BlockSpec(memory_space=pl.ANY)
    result = pl.pallas_call(
        functools.partial(kernel, sizes),
        out_shape=jax.ShapeDtypeStruct((questions, passages), F32),
        in_specs=[hbm] * 12,
        out_specs=vmem,
        scratch_shapes=[
            pltpu.VMEM((texts, seq), jnp.int32),
            pltpu.VMEM((1, n_corpus * texts), jnp.int32),
            pltpu.VMEM((1, n_corpus * texts), jnp.int32),
            pltpu.VMEM((questions, width), BF16),
            pltpu.VMEM((width // 128, 128), F32),
            pltpu.VMEM((width // 128, 128), F32),
            pltpu.VMEM((total, width), BF16),
            pltpu.VMEM((3 * inner, width), BF16),
            pltpu.VMEM((n_tensor, inner, width), BF16),
            pltpu.VMEM((width, ff_here), BF16),
            pltpu.VMEM((ff_here, width), BF16),
            pltpu.VMEM((passages, width), BF16),
            pltpu.VMEM((width, passages), BF16),
            pltpu.VMEM((3 * inner, total), BF16),
            pltpu.VMEM((n_tensor, pieces, inner, PIECE), BF16),
            pltpu.VMEM((PIECE, width), BF16),
            pltpu.VMEM((PIECE, ff_here), BF16),
            pltpu.VMEM((ny, PIECE, width), BF16),
            pltpu.VMEM((ny, PIECE, width), BF16),
            pltpu.VMEM((2, PIECE // 2, width), BF16),
            pltpu.VMEM((2, PIECE // 2, width), F32),
            pltpu.VMEM((n_tensor * n_corpus, 1, width), F32),
            pltpu.VMEM((n_tensor, 1, 128), F32),
            pltpu.VMEM((n_corpus, 1, 128), F32),
            pltpu.VMEM((n_tensor * n_corpus, 1, 128), F32),
            dma((12,)),
            dma((ny,)), dma((ny,)), dma((ny, 3)), dma((2,)), dma((2,)), dma,
            dma((pieces, ny)), dma((pieces, ny)), dma((ny, 2)), dma((ny,)), dma((2,)),
            dma((ny,)), dma, dma((nc,)), dma,
            dma((n_tensor * n_corpus - 1,)), dma,
            dma((n_tensor * n_corpus - 1,)), dma,
            pltpu.SemaphoreType.REGULAR((3,)),
        ],
        compiler_params=pltpu.CompilerParams(
            collective_id=0, has_side_effects=True, vmem_limit_bytes=60 * 1024 * 1024
        ),
        name="hop_two",
    )(
        token_ids[0], hop_passages, path_question, question_vecs[0],
        gain_attn.reshape(-1, 128), gain_out.reshape(-1, 128),
        states.reshape(total, width), jnp.transpose(w_qkv, (1, 2, 0)).reshape(3 * inner, width),
        w_out, w_up, w_down, passage_slab,
    )
    return result[None]


def solution(mesh):
    mesh_sizes = (mesh.shape["corpus"], mesh.shape["batch"], mesh.shape["tensor"])
    return jax.shard_map(
        functools.partial(shards, mesh_sizes),
        mesh=mesh,
        in_specs=(
            P("batch", "corpus", None, None),
            P("batch", "corpus", None),
            P("batch", None),
            P("batch", None),
            P("batch", None, None),
            P(("corpus", "tensor"), None),
            P(None, None, "tensor"),
            P("tensor", None),
            P(None, "tensor"),
            P("tensor", None),
            P(),
            P(),
        ),
        out_specs=P("batch", None, ("corpus", "tensor")),
        check_vma=False,
    )
```

```python
import functools

import jax
import jax.numpy as jnp
from jax import lax
from jax.experimental import pallas as pl
from jax.experimental.pallas import tpu as pltpu
from jax.sharding import PartitionSpec as P

HEAD_DIM = 64
HOPS = 4
PIECE = 128
MESH = pl.DeviceIdType.MESH
F32 = jnp.float32
BF16 = jnp.bfloat16

epsilon = 1e-05
score_gain = 3.0


def dot(a, b, ca, cb):
    return lax.dot_general(a, b, (((ca,), (cb,)), ((), ())), preferred_element_type=F32)


def layer_norm(values, scale_row):
    centered = values - jnp.mean(values, axis=-1, keepdims=True)
    spread = jnp.mean(centered * centered, axis=-1, keepdims=True)
    return centered * lax.rsqrt(spread + epsilon) * scale_row


def gelu(v):
    return 0.5 * v * (1.0 + lax.erf(v * (0.5 ** 0.5)))


def iota(shape, dim):
    return lax.broadcasted_iota(jnp.int32, shape, dim)


def col_to_row(col, width):
    n = col.shape[0]
    same = iota((n, width), 0) == iota((n, width), 1)
    return jnp.sum(jnp.where(same, col, jnp.zeros_like(col)), axis=0, keepdims=True)


def row_to_col(row, n):
    width = row.shape[1]
    same = iota((n, width), 0) == iota((n, width), 1)
    return jnp.sum(jnp.where(same, row, jnp.zeros_like(row)), axis=1, keepdims=True)


def kernel(
    sizes,
    tok_hbm, hop_hbm, pq_hbm, qv_hbm, gain_a_hbm, gain_o_hbm,
    x_hbm, wqkv_hbm, wout_hbm, wup_hbm, wdown_hbm, slab_hbm,
    out_ref,
    tok_ref, hop_ref, pq_ref, qv_ref, gain_a_ref, gain_o_ref,
    x, wqkv, wout, wup, wdown, slab, slab_t,
    qkv, ctx, hid, act, ffp, ffr, opp, partial, pool, hop_y, hop_c, lse,
    load_sem, w1s, w1r, w2s, w2r, w3s, w3r, cs, cr, fs, fr, oppr,
    hys, hyr, hcs, hcr, ps, pr, ls, lr, known,
):
    n_corpus, n_batch, n_tensor, texts, seq, width = sizes
    c = lax.axis_index("corpus")
    b = lax.axis_index("batch")
    t = lax.axis_index("tensor")
    core = lax.rem(c, 2)
    sibling = c + 1 - 2 * core
    heads_here = wqkv.shape[0] // (3 * HEAD_DIM)
    inner = heads_here * HEAD_DIM
    ff_here = wup.shape[1]
    passages = slab.shape[0]
    questions = qv_ref.shape[0]
    paths = n_corpus * texts
    piece = ctx.shape[-1]
    own_pass = (c * n_tensor + t) * passages

    def y_peer(d):
        return (c, b, lax.rem(t + d, n_tensor))

    def c_peer(e, d=0):
        return (lax.rem(c + e, n_corpus), b, lax.rem(t + d, n_tensor))

    def x_peer(f):
        return (c, lax.rem(b + f, n_batch), t)

    def chips_away(e):
        return min(e // 2, (n_corpus - e) // 2)

    def remote(src, dst, s, r, dev):
        return pltpu.make_async_remote_copy(
            src_ref=src, dst_ref=dst, send_sem=s, recv_sem=r, device_id=dev, device_id_type=MESH
        )

    def wait_all(buf, sem):
        there = buf.at[pl.ds(1, buf.shape[0] - 1)]
        remote(there, there, sem, sem, y_peer(1)).wait_recv()

    far_first = sorted(range(1, n_corpus), key=lambda e: -chips_away(e))
    far_first_all = sorted(
        [(e, d) for e in range(n_corpus) for d in range(n_tensor) if e or d],
        key=lambda p: -chips_away(p[0]) - min(p[1], n_tensor - p[1]),
    )

    barrier = pltpu.get_barrier_semaphore()
    peers = [y_peer(d) for d in range(1, n_tensor)] + [(sibling, b, lax.rem(t + d, n_tensor)) for d in range(n_tensor)]
    peers += [c_peer(2), c_peer(n_corpus - 2), x_peer(1), x_peer(n_batch - 1)]
    for dev in peers:
        pl.semaphore_signal(barrier, inc=1, device_id=dev, device_id_type=MESH)

    def tell(stage, chips):
        for e in (2 * chips, n_corpus - 2 * chips):
            pl.semaphore_signal(known.at[stage], inc=1, device_id=c_peer(e), device_id_type=MESH)

    loads = []
    for i, (src, dst) in enumerate((
        (x_hbm, x), (wqkv_hbm, wqkv), (wout_hbm, wout.at[0]), (tok_hbm, tok_ref), (gain_a_hbm, gain_a_ref),
        (gain_o_hbm, gain_o_ref), (hop_hbm, hop_ref), (pq_hbm, pq_ref), (qv_hbm, qv_ref),
        (slab_hbm, slab), (wup_hbm, wup), (wdown_hbm, wdown),
    )):
        loads.append(pltpu.make_async_copy(src, dst, load_sem.at[i]))
    load_x, load_qkv = loads[:2]
    load_small = loads[2:9]
    load_slab, load_up, load_down = loads[9:]
    for copy in loads[:9]:
        copy.start()
    pl.semaphore_wait(barrier, len(peers))

    half = width // 2
    half_cols = pl.ds(pl.multiple_of(core * half, 128), half)
    other_cols = pl.ds(pl.multiple_of((1 - core) * half, 128), half)
    odd = lax.rem(b, 2)
    quarter = inner // 4
    own_rows = pl.ds(pl.multiple_of(odd * 2 * quarter, 16), 2 * quarter)
    own_part = [pl.ds(pl.multiple_of(odd * 2 * quarter + k * quarter, 16), quarter) for k in range(2)]
    next_part = [pl.ds(pl.multiple_of((1 - odd) * 2 * quarter + k * quarter, 16), quarter) for k in range(2)]
    leg1 = [
        remote(wout_hbm.at[own_rows, half_cols], wout.at[d, own_rows, half_cols], w1s.at[d - 1], w1r.at[d - 1], y_peer(d))
        for d in range(1, n_tensor)
    ]
    for copy in leg1:
        copy.start()
    tell(0, 1)

    load_x.wait()
    load_qkv.wait()
    for copy in (load_slab, load_up, load_down):
        copy.start()
    qkv[...] = dot(wqkv[...], x[...], 1, 1).astype(BF16)
    for copy in load_small:
        copy.wait()
    gain_a = jnp.concatenate([gain_a_ref[r:r + 1, :] for r in range(width // 128)], axis=1)
    gain_o = jnp.concatenate([gain_o_ref[r:r + 1, :] for r in range(width // 128)], axis=1)
    real = tok_ref[...] != 1
    counts = jnp.sum(real.astype(F32), axis=1, keepdims=True)

    split = seq // piece
    for i in range(texts):
        cols = slice(i * seq, (i + 1) * seq)
        keep = iota((seq, 1), 0).astype(F32) < counts[i:i + 1, :]
        for h in range(heads_here):
            lo = h * HEAD_DIM
            q = qkv[lo:lo + HEAD_DIM, cols] * jnp.asarray(HEAD_DIM ** -0.5, BF16)
            k = qkv[inner + lo:inner + lo + HEAD_DIM, cols]
            v = qkv[2 * inner + lo:2 * inner + lo + HEAD_DIM, cols]
            logits = dot(k, q, 0, 0)
            logits = jnp.where(keep, logits, -jnp.inf)
            weights = jnp.exp(logits - jnp.max(logits, axis=0, keepdims=True))
            weights = (weights * (1.0 / jnp.sum(weights, axis=0, keepdims=True))).astype(BF16)
            context = dot(v, weights, 1, 0).astype(BF16)
            for j in range(split):
                ctx[0, i * split + j, lo:lo + HEAD_DIM, :] = context[:, j * piece:(j + 1) * piece]
    steps = (2, 1, 3, 0)
    ctx_sends = {}
    for k in steps:
        ctx_sends[k] = []
        for d in range(1, n_tensor):
            q = lax.rem(t + d + k, n_tensor)
            ctx_sends[k].append(remote(ctx.at[0, q], ctx.at[d, k], cs.at[k, d - 1], cr.at[k, d - 1], y_peer(d)))

    def issue(p):
        for copy in ctx_sends[p]:
            copy.start()

    pl.semaphore_wait(known.at[0], 2)
    tell(1, 2)

    issue(2)
    issue(1)
    load_slab.wait()
    pq = pq_ref[...]
    member = iota((questions, paths), 0) == pq
    before = jnp.sum((pq < iota((questions, paths), 0)).astype(F32), axis=1, keepdims=True)
    amount = jnp.sum(member.astype(F32), axis=1, keepdims=True)
    hop_col = row_to_col(hop_ref[...].astype(F32), paths)
    here = iota((paths, passages), 1).astype(F32) == hop_col - own_pass.astype(F32)
    picked = dot(here.astype(F32).astype(BF16), slab[...], 1, 0)
    question_rows = dot(member.astype(F32).astype(BF16), qv_ref[...], 0, 0)
    hop_y[0] = col_to_row(jnp.sum(picked * question_rows, axis=1, keepdims=True), 128)
    hop_sends = [
        remote(hop_y.at[0], hop_y.at[d], hys.at[d - 1], hyr, y_peer(d)) for d in range(1, n_tensor)
    ]
    for copy in hop_sends:
        copy.start()

    leg2 = []
    for d in (1, n_tensor - 1, 2):
        if d == 2:
            pl.semaphore_wait(known.at[1], 2)
            tell(2, 1)
        leg1[d - 1].wait_recv()
        group = [
            remote(wout.at[d, own_part[k], half_cols], wout.at[d, own_part[k], half_cols], w2s.at[d - 1, k], w2r.at[k], x_peer(f))
            for k, f in ((0, 1), (1, n_batch - 1))
        ]
        group.append(remote(wout.at[d, own_rows, half_cols], wout.at[d, own_rows, half_cols], w2s.at[d - 1, 2], w3r, (sibling, b, t)))
        for copy in group:
            copy.start()
        leg2 += group
        if d == 2:
            issue(3)
            issue(0)
    for n in range(0, passages, 256):
        slab_t[:, n:n + 256] = slab[n:n + 256, :].T
    load_up.wait()
    load_down.wait()

    for k, f in ((0, 1), (1, n_batch - 1)):
        there = wout.at[1:n_tensor, next_part[k], half_cols]
        remote(there, there, w2s.at[0, k], w2r.at[k], x_peer(f)).wait_recv()
        copy = remote(there, there, w3s.at[k], w3r, (sibling, b, t))
        copy.start()
        leg2.append(copy)
    there = wout.at[1:n_tensor, :, other_cols]
    remote(there, there, w3s.at[0], w3r, (sibling, b, t)).wait_recv()


    ff_sends = []
    halves = (slice(0, piece // 2), slice(piece // 2, piece))
    for k in steps:
        q = lax.rem(t + k, n_tensor)
        attended = x[pl.ds(pl.multiple_of(q * piece, 16), piece), :].astype(F32)
        attended = attended + dot(ctx[0, q], wout[0], 0, 0)
        for d in range(1, n_tensor):
            ctx_sends[k][d - 1].wait_recv()
            attended = attended + dot(ctx[d, k], wout[d], 0, 0)
        hidden = layer_norm(attended, gain_a).astype(BF16)
        hid[...] = hidden
        for n in range(0, ff_here, 256):
            up = dot(hid[...], wup[:, n:n + 256], 1, 0)
            act[:, n:n + 256] = gelu(up).astype(BF16)
        down = dot(act[...], wdown[...], 1, 0)
        if k == 2:
            ffp[1] = down.astype(BF16)
            for r, f in ((0, 1), (1, n_tensor - 1)):
                ff_sends.append(remote(ffp.at[1, halves[r]], opp.at[r], fs.at[1, r], oppr.at[r], y_peer(f)))
                ff_sends[-1].start()
        elif k:
            late = 0 if k == 1 else 1
            ffp[k - 1, halves[1 - late], :] = down[halves[1 - late], :].astype(BF16)
            partial[late] = down[halves[late], :]
            part = halves[1 - late]
            ff_sends.append(remote(ffp.at[k - 1, part], ffr.at[k - 1, part], fs.at[k - 1, 1 - late], fr.at[k - 1], y_peer(k)))
            ff_sends[-1].start()
        if k == steps[0]:
            pl.semaphore_wait(known.at[2], 2)
            wait_all(hop_y, hyr)
            hop_c[0] = jnp.sum(hop_y[...], axis=0)
            hopc_sends = [
                remote(hop_c.at[0], hop_c.at[e], hcs.at[e - 1], hcr, c_peer(e)) for e in far_first
            ]
            for copy in hopc_sends:
                copy.start()

    for late, k in ((0, 1), (1, n_tensor - 1)):
        part = halves[late]
        ff_sends[late].wait_recv()
        ffp[k - 1, part, :] = (partial[late] + opp[late].astype(F32)).astype(BF16)
        ff_sends.append(remote(ffp.at[k - 1, part], ffr.at[k - 1, part], fs.at[k - 1, late], fr.at[k - 1], y_peer(k)))
        ff_sends[-1].start()
    total = hid[...].astype(F32) + down
    for k in (1, n_tensor - 1):
        remote(ffr.at[k - 1], ffr.at[k - 1], fs.at[k - 1, 0], fr.at[k - 1], y_peer(k)).wait_recv()
        total = total + ffr[k - 1].astype(F32)
    encoded = layer_norm(total, gain_o)
    own_count = sum(jnp.where(t // split == i, counts[i:i + 1, :], 0.0) for i in range(texts))
    keep = (lax.rem(t, split) * piece + iota((piece, 1), 0)).astype(F32) < own_count
    me = c * n_tensor + t
    pool[pl.ds(me, 1)] = (jnp.sum(jnp.where(keep, encoded, 0.0), axis=0, keepdims=True) / own_count)[None]
    pool_sends = [
        remote(pool.at[me], pool.at[me], ps.at[k], pr, c_peer(e, d)) for k, (e, d) in enumerate(far_first_all)
    ]
    for copy in pool_sends:
        copy.start()

    wait_all(hop_c, hcr)
    hop_row = jnp.sum(hop_c[...], axis=0)[:, :paths]
    path_at = iota((questions, paths), 1).astype(F32)
    hops, picks = [], []
    for k in range(HOPS):
        ok = amount > k
        hop = jnp.sum(jnp.where(path_at == before + k, hop_row, 0.0), axis=1, keepdims=True)
        hops.append(jnp.where(ok, hop, -jnp.inf))
        picks.append(jnp.where((path_at == before + k) & ok, 1.0, 0.0))
    pick = jnp.concatenate(picks, axis=0).astype(BF16)

    others = pool.at[pl.ds(0, n_corpus * n_tensor - 1)]
    remote(others, others, ps.at[0], pr, y_peer(1)).wait_recv()
    pooled = jnp.sum(pool[...].reshape(paths, split, 1, width), axis=1).reshape(paths, width)
    pooled = pooled.astype(BF16).astype(F32)
    queries = (pooled * lax.rsqrt(jnp.sum(pooled * pooled, axis=-1, keepdims=True) + 1e-06)).astype(BF16)
    chosen = dot(pick, queries, 1, 0).astype(BF16)
    direct = dot(chosen, slab_t[...], 1, 0)
    scores = [hops[k] + score_gain * direct[k * questions:(k + 1) * questions] for k in range(HOPS)]
    top = functools.reduce(jnp.maximum, scores)
    inner_sum = sum(jnp.exp(s - top) for s in scores)
    local_top = jnp.max(top, axis=1, keepdims=True)
    local_sum = jnp.sum(inner_sum * jnp.exp(top - local_top), axis=1, keepdims=True)
    local_lse = local_top + jnp.log(local_sum)

    lse[0] = col_to_row(local_lse, 128)
    lse_sends = [
        remote(lse.at[0], lse.at[k + 1], ls.at[k], lr, c_peer(e, d)) for k, (e, d) in enumerate(far_first_all)
    ]
    for copy in lse_sends:
        copy.start()
    marginal = top + jnp.log(inner_sum)
    wait_all(lse, lr)
    parts = lse[...]
    most = jnp.max(parts, axis=0)
    norm = most + jnp.log(jnp.sum(jnp.exp(parts - most[None]), axis=0))
    out_ref[...] = marginal - row_to_col(norm, questions)

    for group in [leg1, leg2, hop_sends, hopc_sends, pool_sends, lse_sends, ff_sends] + list(ctx_sends.values()):
        for copy in group:
            copy.wait_send()


def shards(mesh_sizes, states, token_ids, hop_passages, path_question, question_vecs, passage_slab,
           w_qkv, w_out, w_up, w_down, gain_attn, gain_out):
    n_corpus, n_batch, n_tensor = mesh_sizes
    texts, seq, width = states.shape[1:]
    total = texts * seq
    passages = passage_slab.shape[0]
    questions = question_vecs.shape[1]
    inner = w_qkv.shape[2]
    ff_here = w_up.shape[1]
    sizes = (n_corpus, n_batch, n_tensor, texts, seq, width)
    ny, nc = n_tensor - 1, n_corpus - 1
    pieces = total // PIECE
    dma = pltpu.SemaphoreType.DMA
    vmem = pl.BlockSpec(memory_space=pltpu.VMEM)
    hbm = pl.BlockSpec(memory_space=pl.ANY)
    result = pl.pallas_call(
        functools.partial(kernel, sizes),
        out_shape=jax.ShapeDtypeStruct((questions, passages), F32),
        in_specs=[hbm] * 12,
        out_specs=vmem,
        scratch_shapes=[
            pltpu.VMEM((texts, seq), jnp.int32),
            pltpu.VMEM((1, n_corpus * texts), jnp.int32),
            pltpu.VMEM((1, n_corpus * texts), jnp.int32),
            pltpu.VMEM((questions, width), BF16),
            pltpu.VMEM((width // 128, 128), F32),
            pltpu.VMEM((width // 128, 128), F32),
            pltpu.VMEM((total, width), BF16),
            pltpu.VMEM((3 * inner, width), BF16),
            pltpu.VMEM((n_tensor, inner, width), BF16),
            pltpu.VMEM((width, ff_here), BF16),
            pltpu.VMEM((ff_here, width), BF16),
            pltpu.VMEM((passages, width), BF16),
            pltpu.VMEM((width, passages), BF16),
            pltpu.VMEM((3 * inner, total), BF16),
            pltpu.VMEM((n_tensor, pieces, inner, PIECE), BF16),
            pltpu.VMEM((PIECE, width), BF16),
            pltpu.VMEM((PIECE, ff_here), BF16),
            pltpu.VMEM((ny, PIECE, width), BF16),
            pltpu.VMEM((ny, PIECE, width), BF16),
            pltpu.VMEM((2, PIECE // 2, width), BF16),
            pltpu.VMEM((2, PIECE // 2, width), F32),
            pltpu.VMEM((n_tensor * n_corpus, 1, width), F32),
            pltpu.VMEM((n_tensor, 1, 128), F32),
            pltpu.VMEM((n_corpus, 1, 128), F32),
            pltpu.VMEM((n_tensor * n_corpus, 1, 128), F32),
            dma((12,)),
            dma((ny,)), dma((ny,)), dma((ny, 3)), dma((2,)), dma((2,)), dma,
            dma((pieces, ny)), dma((pieces, ny)), dma((ny, 2)), dma((ny,)), dma((2,)),
            dma((ny,)), dma, dma((nc,)), dma,
            dma((n_tensor * n_corpus - 1,)), dma,
            dma((n_tensor * n_corpus - 1,)), dma,
            pltpu.SemaphoreType.REGULAR((3,)),
        ],
        compiler_params=pltpu.CompilerParams(
            collective_id=0, has_side_effects=True, vmem_limit_bytes=60 * 1024 * 1024
        ),
        name="hop_two",
    )(
        token_ids[0], hop_passages, path_question, question_vecs[0],
        gain_attn.reshape(-1, 128), gain_out.reshape(-1, 128),
        states.reshape(total, width), jnp.transpose(w_qkv, (1, 2, 0)).reshape(3 * inner, width),
        w_out, w_up, w_down, passage_slab,
    )
    return result[None]


def solution(mesh):
    mesh_sizes = (mesh.shape["corpus"], mesh.shape["batch"], mesh.shape["tensor"])
    return jax.shard_map(
        functools.partial(shards, mesh_sizes),
        mesh=mesh,
        in_specs=(
            P("batch", "corpus", None, None),
            P("batch", "corpus", None),
            P("batch", None),
            P("batch", None),
            P("batch", None, None),
            P(("corpus", "tensor"), None),
            P(None, None, "tensor"),
            P("tensor", None),
            P(None, "tensor"),
            P("tensor", None),
            P(),
            P(),
        ),
        out_specs=P("batch", None, ("corpus", "tensor")),
        check_vma=False,
    )
```

```python
import functools

import jax
import jax.numpy as jnp
from jax import lax
from jax.experimental import pallas as pl
from jax.experimental.pallas import tpu as pltpu
from jax.sharding import PartitionSpec as P

HEAD_DIM = 64
HOPS = 4
PIECE = 128
MESH = pl.DeviceIdType.MESH
F32 = jnp.float32
BF16 = jnp.bfloat16

epsilon = 1e-05
score_gain = 3.0


def dot(a, b, ca, cb):
    return lax.dot_general(a, b, (((ca,), (cb,)), ((), ())), preferred_element_type=F32)


def layer_norm(values, scale_row):
    centered = values - jnp.mean(values, axis=-1, keepdims=True)
    spread = jnp.mean(centered * centered, axis=-1, keepdims=True)
    return centered * lax.rsqrt(spread + epsilon) * scale_row


def gelu(v):
    return 0.5 * v * (1.0 + lax.erf(v * (0.5 ** 0.5)))


def iota(shape, dim):
    return lax.broadcasted_iota(jnp.int32, shape, dim)


def col_to_row(col, width):
    n = col.shape[0]
    same = iota((n, width), 0) == iota((n, width), 1)
    return jnp.sum(jnp.where(same, col, jnp.zeros_like(col)), axis=0, keepdims=True)


def row_to_col(row, n):
    width = row.shape[1]
    same = iota((n, width), 0) == iota((n, width), 1)
    return jnp.sum(jnp.where(same, row, jnp.zeros_like(row)), axis=1, keepdims=True)


def kernel(
    sizes,
    tok_hbm, hop_hbm, pq_hbm, qv_hbm, gain_a_hbm, gain_o_hbm,
    x_hbm, wqkv_hbm, wout_hbm, wup_hbm, wdown_hbm, slab_hbm,
    out_ref,
    tok_ref, hop_ref, pq_ref, qv_ref, gain_a_ref, gain_o_ref,
    x, wqkv, wout, wup, wdown, slab, slab_t,
    qkv, ctx, hid, act, ffp, ffr, opp, partial, pool, hop_y, hop_c, lse,
    load_sem, w1s, w1r, w2s, w2r, w3s, w3r, cs, cr, fs, fr, oppr,
    hys, hyr, hcs, hcr, ps, pr, ls, lr, known,
):
    n_corpus, n_batch, n_tensor, texts, seq, width = sizes
    c = lax.axis_index("corpus")
    b = lax.axis_index("batch")
    t = lax.axis_index("tensor")
    core = lax.rem(c, 2)
    sibling = c + 1 - 2 * core
    heads_here = wqkv.shape[0] // (3 * HEAD_DIM)
    inner = heads_here * HEAD_DIM
    ff_here = wup.shape[1]
    passages = slab.shape[0]
    questions = qv_ref.shape[0]
    paths = n_corpus * texts
    piece = ctx.shape[-1]
    own_pass = (c * n_tensor + t) * passages

    def y_peer(d):
        return (c, b, lax.rem(t + d, n_tensor))

    def c_peer(e, d=0):
        return (lax.rem(c + e, n_corpus), b, lax.rem(t + d, n_tensor))

    def x_peer(f):
        return (c, lax.rem(b + f, n_batch), t)

    def chips_away(e):
        return min(e // 2, (n_corpus - e) // 2)

    def remote(src, dst, s, r, dev):
        return pltpu.make_async_remote_copy(
            src_ref=src, dst_ref=dst, send_sem=s, recv_sem=r, device_id=dev, device_id_type=MESH
        )

    def wait_all(buf, sem):
        there = buf.at[pl.ds(1, buf.shape[0] - 1)]
        remote(there, there, sem, sem, y_peer(1)).wait_recv()

    far_first = sorted(range(1, n_corpus), key=lambda e: -chips_away(e))
    far_first_all = sorted(
        [(e, d) for e in range(n_corpus) for d in range(n_tensor) if e or d],
        key=lambda p: -chips_away(p[0]) - min(p[1], n_tensor - p[1]),
    )

    barrier = pltpu.get_barrier_semaphore()
    peers = [y_peer(d) for d in range(1, n_tensor)] + [(sibling, b, lax.rem(t + d, n_tensor)) for d in range(n_tensor)]
    peers += [c_peer(2), c_peer(n_corpus - 2), x_peer(1), x_peer(n_batch - 1)]
    for dev in peers:
        pl.semaphore_signal(barrier, inc=1, device_id=dev, device_id_type=MESH)

    def tell(stage, chips):
        for e in (2 * chips, n_corpus - 2 * chips):
            pl.semaphore_signal(known.at[stage], inc=1, device_id=c_peer(e), device_id_type=MESH)

    loads = []
    for i, (src, dst) in enumerate((
        (x_hbm, x), (wqkv_hbm, wqkv), (wout_hbm, wout.at[0]), (tok_hbm, tok_ref), (gain_a_hbm, gain_a_ref),
        (gain_o_hbm, gain_o_ref), (hop_hbm, hop_ref), (pq_hbm, pq_ref), (qv_hbm, qv_ref),
        (slab_hbm, slab), (wup_hbm, wup), (wdown_hbm, wdown),
    )):
        loads.append(pltpu.make_async_copy(src, dst, load_sem.at[i]))
    load_x, load_qkv = loads[:2]
    load_small = loads[2:9]
    load_slab, load_up, load_down = loads[9:]
    for copy in loads[:9]:
        copy.start()
    pl.semaphore_wait(barrier, len(peers))

    half = width // 2
    half_cols = pl.ds(pl.multiple_of(core * half, 128), half)
    other_cols = pl.ds(pl.multiple_of((1 - core) * half, 128), half)
    odd = lax.rem(b, 2)
    quarter = inner // 4
    own_rows = pl.ds(pl.multiple_of(odd * 2 * quarter, 16), 2 * quarter)
    own_part = [pl.ds(pl.multiple_of(odd * 2 * quarter + k * quarter, 16), quarter) for k in range(2)]
    next_part = [pl.ds(pl.multiple_of((1 - odd) * 2 * quarter + k * quarter, 16), quarter) for k in range(2)]
    leg1 = [
        remote(wout_hbm.at[own_rows, half_cols], wout.at[d, own_rows, half_cols], w1s.at[d - 1], w1r.at[d - 1], y_peer(d))
        for d in range(1, n_tensor)
    ]
    for copy in leg1:
        copy.start()
    tell(0, 1)

    load_x.wait()
    load_qkv.wait()
    for copy in (load_slab, load_up, load_down):
        copy.start()
    qkv[...] = dot(wqkv[...], x[...], 1, 1).astype(BF16)
    for copy in load_small:
        copy.wait()
    gain_a = jnp.concatenate([gain_a_ref[r:r + 1, :] for r in range(width // 128)], axis=1)
    gain_o = jnp.concatenate([gain_o_ref[r:r + 1, :] for r in range(width // 128)], axis=1)
    real = tok_ref[...] != 1
    counts = jnp.sum(real.astype(F32), axis=1, keepdims=True)

    split = seq // piece
    for i in range(texts):
        cols = slice(i * seq, (i + 1) * seq)
        keep = iota((seq, 1), 0).astype(F32) < counts[i:i + 1, :]
        for h in range(heads_here):
            lo = h * HEAD_DIM
            q = qkv[lo:lo + HEAD_DIM, cols] * jnp.asarray(HEAD_DIM ** -0.5, BF16)
            k = qkv[inner + lo:inner + lo + HEAD_DIM, cols]
            v = qkv[2 * inner + lo:2 * inner + lo + HEAD_DIM, cols]
            logits = dot(k, q, 0, 0)
            logits = jnp.where(keep, logits, -jnp.inf)
            weights = jnp.exp(logits - jnp.max(logits, axis=0, keepdims=True))
            weights = (weights * (1.0 / jnp.sum(weights, axis=0, keepdims=True))).astype(BF16)
            context = dot(v, weights, 1, 0).astype(BF16)
            for j in range(split):
                ctx[0, i * split + j, lo:lo + HEAD_DIM, :] = context[:, j * piece:(j + 1) * piece]
    steps = (2, 1, 3, 0)
    ctx_sends = {}
    for k in steps:
        ctx_sends[k] = []
        for d in range(1, n_tensor):
            q = lax.rem(t + d + k, n_tensor)
            ctx_sends[k].append(remote(ctx.at[0, q], ctx.at[d, k], cs.at[k, d - 1], cr.at[k, d - 1], y_peer(d)))

    def issue(p):
        for copy in ctx_sends[p]:
            copy.start()

    pl.semaphore_wait(known.at[0], 2)
    tell(1, 2)

    issue(2)
    issue(1)
    load_slab.wait()
    pq = pq_ref[...]
    member = iota((questions, paths), 0) == pq
    before = jnp.sum((pq < iota((questions, paths), 0)).astype(F32), axis=1, keepdims=True)
    amount = jnp.sum(member.astype(F32), axis=1, keepdims=True)
    hop_col = row_to_col(hop_ref[...].astype(F32), paths)
    here = iota((paths, passages), 1).astype(F32) == hop_col - own_pass.astype(F32)
    picked = dot(here.astype(F32).astype(BF16), slab[...], 1, 0)
    question_rows = dot(member.astype(F32).astype(BF16), qv_ref[...], 0, 0)
    hop_y[0] = col_to_row(jnp.sum(picked * question_rows, axis=1, keepdims=True), 128)
    hop_sends = [
        remote(hop_y.at[0], hop_y.at[d], hys.at[d - 1], hyr, y_peer(d)) for d in range(1, n_tensor)
    ]
    for copy in hop_sends:
        copy.start()

    leg2 = []
    for d in (1, n_tensor - 1, 2):
        if d == 2:
            pl.semaphore_wait(known.at[1], 2)
            tell(2, 1)
        leg1[d - 1].wait_recv()
        group = [
            remote(wout.at[d, own_part[k], half_cols], wout.at[d, own_part[k], half_cols], w2s.at[d - 1, k], w2r.at[k], x_peer(f))
            for k, f in ((0, 1), (1, n_batch - 1))
        ]
        group.append(remote(wout.at[d, own_rows, half_cols], wout.at[d, own_rows, half_cols], w2s.at[d - 1, 2], w3r, (sibling, b, t)))
        for copy in group:
            copy.start()
        leg2 += group
        if d == 2:
            issue(3)
            issue(0)
    for n in range(0, passages, 256):
        slab_t[:, n:n + 256] = slab[n:n + 256, :].T
    load_up.wait()
    load_down.wait()

    for k, f in ((0, 1), (1, n_batch - 1)):
        there = wout.at[1:n_tensor, next_part[k], half_cols]
        remote(there, there, w2s.at[0, k], w2r.at[k], x_peer(f)).wait_recv()
        copy = remote(there, there, w3s.at[k], w3r, (sibling, b, t))
        copy.start()
        leg2.append(copy)
    there = wout.at[1:n_tensor, :, other_cols]
    remote(there, there, w3s.at[0], w3r, (sibling, b, t)).wait_recv()


    ff_sends = []
    halves = (slice(0, piece // 2), slice(piece // 2, piece))
    for k in steps:
        q = lax.rem(t + k, n_tensor)
        attended = x[pl.ds(pl.multiple_of(q * piece, 16), piece), :].astype(F32)
        attended = attended + dot(ctx[0, q], wout[0], 0, 0)
        for d in range(1, n_tensor):
            ctx_sends[k][d - 1].wait_recv()
            attended = attended + dot(ctx[d, k], wout[d], 0, 0)
        hidden = layer_norm(attended, gain_a).astype(BF16)
        hid[...] = hidden
        for n in range(0, ff_here, 256):
            up = dot(hid[...], wup[:, n:n + 256], 1, 0)
            act[:, n:n + 256] = gelu(up).astype(BF16)
        down = dot(act[...], wdown[...], 1, 0)
        if k == 2:
            ffp[1] = down.astype(BF16)
            for r, f in ((0, 1), (1, n_tensor - 1)):
                ff_sends.append(remote(ffp.at[1, halves[r]], opp.at[r], fs.at[1, r], oppr.at[r], y_peer(f)))
                ff_sends[-1].start()
        elif k:
            late = 0 if k == 1 else 1
            ffp[k - 1, halves[1 - late], :] = down[halves[1 - late], :].astype(BF16)
            partial[late] = down[halves[late], :]
            part = halves[1 - late]
            ff_sends.append(remote(ffp.at[k - 1, part], ffr.at[k - 1, part], fs.at[k - 1, 1 - late], fr.at[k - 1], y_peer(k)))
            ff_sends[-1].start()
        if k == steps[-1]:
            pl.semaphore_wait(known.at[2], 2)
            wait_all(hop_y, hyr)
            hop_c[0] = jnp.sum(hop_y[...], axis=0)
            hopc_sends = [
                remote(hop_c.at[0], hop_c.at[e], hcs.at[e - 1], hcr, c_peer(e)) for e in far_first
            ]
            for copy in hopc_sends:
                copy.start()

    for late, k in ((0, 1), (1, n_tensor - 1)):
        part = halves[late]
        ff_sends[late].wait_recv()
        ffp[k - 1, part, :] = (partial[late] + opp[late].astype(F32)).astype(BF16)
        ff_sends.append(remote(ffp.at[k - 1, part], ffr.at[k - 1, part], fs.at[k - 1, late], fr.at[k - 1], y_peer(k)))
        ff_sends[-1].start()
    total = hid[...].astype(F32) + down
    for k in (1, n_tensor - 1):
        remote(ffr.at[k - 1], ffr.at[k - 1], fs.at[k - 1, 0], fr.at[k - 1], y_peer(k)).wait_recv()
        total = total + ffr[k - 1].astype(F32)
    encoded = layer_norm(total, gain_o)
    own_count = sum(jnp.where(t // split == i, counts[i:i + 1, :], 0.0) for i in range(texts))
    keep = (lax.rem(t, split) * piece + iota((piece, 1), 0)).astype(F32) < own_count
    me = c * n_tensor + t
    pool[pl.ds(me, 1)] = (jnp.sum(jnp.where(keep, encoded, 0.0), axis=0, keepdims=True) / own_count)[None]
    pool_sends = [
        remote(pool.at[me], pool.at[me], ps.at[k], pr, c_peer(e, d)) for k, (e, d) in enumerate(far_first_all)
    ]
    for copy in pool_sends:
        copy.start()

    wait_all(hop_c, hcr)
    hop_row = jnp.sum(hop_c[...], axis=0)[:, :paths]
    path_at = iota((questions, paths), 1).astype(F32)
    hops, picks = [], []
    for k in range(HOPS):
        ok = amount > k
        hop = jnp.sum(jnp.where(path_at == before + k, hop_row, 0.0), axis=1, keepdims=True)
        hops.append(jnp.where(ok, hop, -jnp.inf))
        picks.append(jnp.where((path_at == before + k) & ok, 1.0, 0.0))
    pick = jnp.concatenate(picks, axis=0).astype(BF16)

    others = pool.at[pl.ds(0, n_corpus * n_tensor - 1)]
    remote(others, others, ps.at[0], pr, y_peer(1)).wait_recv()
    pooled = jnp.sum(pool[...].reshape(paths, split, 1, width), axis=1).reshape(paths, width)
    pooled = pooled.astype(BF16).astype(F32)
    queries = (pooled * lax.rsqrt(jnp.sum(pooled * pooled, axis=-1, keepdims=True) + 1e-06)).astype(BF16)
    chosen = dot(pick, queries, 1, 0).astype(BF16)
    direct = dot(chosen, slab_t[...], 1, 0)
    scores = [hops[k] + score_gain * direct[k * questions:(k + 1) * questions] for k in range(HOPS)]
    top = functools.reduce(jnp.maximum, scores)
    inner_sum = sum(jnp.exp(s - top) for s in scores)
    local_top = jnp.max(top, axis=1, keepdims=True)
    local_sum = jnp.sum(inner_sum * jnp.exp(top - local_top), axis=1, keepdims=True)
    local_lse = local_top + jnp.log(local_sum)

    lse[0] = col_to_row(local_lse, 128)
    lse_sends = [
        remote(lse.at[0], lse.at[k + 1], ls.at[k], lr, c_peer(e, d)) for k, (e, d) in enumerate(far_first_all)
    ]
    for copy in lse_sends:
        copy.start()
    marginal = top + jnp.log(inner_sum)
    wait_all(lse, lr)
    parts = lse[...]
    most = jnp.max(parts, axis=0)
    norm = most + jnp.log(jnp.sum(jnp.exp(parts - most[None]), axis=0))
    out_ref[...] = marginal - row_to_col(norm, questions)

    for group in [leg1, leg2, hop_sends, hopc_sends, pool_sends, lse_sends, ff_sends] + list(ctx_sends.values()):
        for copy in group:
            copy.wait_send()


def shards(mesh_sizes, states, token_ids, hop_passages, path_question, question_vecs, passage_slab,
           w_qkv, w_out, w_up, w_down, gain_attn, gain_out):
    n_corpus, n_batch, n_tensor = mesh_sizes
    texts, seq, width = states.shape[1:]
    total = texts * seq
    passages = passage_slab.shape[0]
    questions = question_vecs.shape[1]
    inner = w_qkv.shape[2]
    ff_here = w_up.shape[1]
    sizes = (n_corpus, n_batch, n_tensor, texts, seq, width)
    ny, nc = n_tensor - 1, n_corpus - 1
    pieces = total // PIECE
    dma = pltpu.SemaphoreType.DMA
    vmem = pl.BlockSpec(memory_space=pltpu.VMEM)
    hbm = pl.BlockSpec(memory_space=pl.ANY)
    result = pl.pallas_call(
        functools.partial(kernel, sizes),
        out_shape=jax.ShapeDtypeStruct((questions, passages), F32),
        in_specs=[hbm] * 12,
        out_specs=vmem,
        scratch_shapes=[
            pltpu.VMEM((texts, seq), jnp.int32),
            pltpu.VMEM((1, n_corpus * texts), jnp.int32),
            pltpu.VMEM((1, n_corpus * texts), jnp.int32),
            pltpu.VMEM((questions, width), BF16),
            pltpu.VMEM((width // 128, 128), F32),
            pltpu.VMEM((width // 128, 128), F32),
            pltpu.VMEM((total, width), BF16),
            pltpu.VMEM((3 * inner, width), BF16),
            pltpu.VMEM((n_tensor, inner, width), BF16),
            pltpu.VMEM((width, ff_here), BF16),
            pltpu.VMEM((ff_here, width), BF16),
            pltpu.VMEM((passages, width), BF16),
            pltpu.VMEM((width, passages), BF16),
            pltpu.VMEM((3 * inner, total), BF16),
            pltpu.VMEM((n_tensor, pieces, inner, PIECE), BF16),
            pltpu.VMEM((PIECE, width), BF16),
            pltpu.VMEM((PIECE, ff_here), BF16),
            pltpu.VMEM((ny, PIECE, width), BF16),
            pltpu.VMEM((ny, PIECE, width), BF16),
            pltpu.VMEM((2, PIECE // 2, width), BF16),
            pltpu.VMEM((2, PIECE // 2, width), F32),
            pltpu.VMEM((n_tensor * n_corpus, 1, width), F32),
            pltpu.VMEM((n_tensor, 1, 128), F32),
            pltpu.VMEM((n_corpus, 1, 128), F32),
            pltpu.VMEM((n_tensor * n_corpus, 1, 128), F32),
            dma((12,)),
            dma((ny,)), dma((ny,)), dma((ny, 3)), dma((2,)), dma((2,)), dma,
            dma((pieces, ny)), dma((pieces, ny)), dma((ny, 2)), dma((ny,)), dma((2,)),
            dma((ny,)), dma, dma((nc,)), dma,
            dma((n_tensor * n_corpus - 1,)), dma,
            dma((n_tensor * n_corpus - 1,)), dma,
            pltpu.SemaphoreType.REGULAR((3,)),
        ],
        compiler_params=pltpu.CompilerParams(
            collective_id=0, has_side_effects=True, vmem_limit_bytes=60 * 1024 * 1024
        ),
        name="hop_two",
    )(
        token_ids[0], hop_passages, path_question, question_vecs[0],
        gain_attn.reshape(-1, 128), gain_out.reshape(-1, 128),
        states.reshape(total, width), jnp.transpose(w_qkv, (1, 2, 0)).reshape(3 * inner, width),
        w_out, w_up, w_down, passage_slab,
    )
    return result[None]


def solution(mesh):
    mesh_sizes = (mesh.shape["corpus"], mesh.shape["batch"], mesh.shape["tensor"])
    return jax.shard_map(
        functools.partial(shards, mesh_sizes),
        mesh=mesh,
        in_specs=(
            P("batch", "corpus", None, None),
            P("batch", "corpus", None),
            P("batch", None),
            P("batch", None),
            P("batch", None, None),
            P(("corpus", "tensor"), None),
            P(None, None, "tensor"),
            P("tensor", None),
            P(None, "tensor"),
            P("tensor", None),
            P(),
            P(),
        ),
        out_specs=P("batch", None, ("corpus", "tensor")),
        check_vma=False,
    )
```
